32 devices in a mesh: group: 2 (over y), dp: 8 (over z, x), tensor: 2 (over core).
Axes of the slice: x: 2, y: 2, z: 4, core: 2. Of those that a mesh axis runs over, the one named last changes fastest.
Arguments:
- layer_input: bfloat16 [2, 16, 512, 768], P(None, ('group', 'dp'), 'tensor'), may hold values from -6 to 6
- out_cotangent: bfloat16 [2, 16, 512, 768], P(None, ('group', 'dp'), 'tensor'), may hold values from -6 to 6
- lengths: int32 [2, 16], P(None, ('group', 'dp')), may hold values from 128 to 512, as said below
- global_blocks: int32 [2, 16, 2], P(None, ('group', 'dp')), may hold values from 0 to 7, as said below
- rand_blocks: int32 [2, 16, 8, 12, 3], P(None, ('group', 'dp'), None, 'tensor'), may hold values from 0 to 7, as said below
- inner_steps: int32 [2], P('group'), may hold values from 1 to 20
- wide_inner: float32 [2, 1, 768, 2, 2688], P('group', None, 'dp', 'tensor'), may hold values from -0.21875 to 0.21875
- wide_first: float32 [2, 1, 768, 2, 2688], P('group', None, 'dp', 'tensor'), may hold values from -19.00703 to 19.00703
- wide_second: float32 [2, 1, 768, 2, 2688], P('group', None, 'dp', 'tensor'), may hold values from 0.8192 to 8.192
- wide_anchor: float32 [1, 768, 2, 2688], P(None, 'dp', 'tensor'), may hold values from -0.21875 to 0.21875
- wide_outer: float32 [1, 768, 2, 2688], P(None, 'dp', 'tensor'), may hold values from -0.06 to 0.06
- narrow_inner: float32 [2, 1, 2, 1920, 768], P('group', None, 'tensor', 'dp'), may hold values from -0.21875 to 0.21875
- narrow_first: float32 [2, 1, 2, 1920, 768], P('group', None, 'tensor', 'dp'), may hold values from -19.00703 to 19.00703
- narrow_second: float32 [2, 1, 2, 1920, 768], P('group', None, 'tensor', 'dp'), may hold values from 0.8192 to 8.192
- narrow_anchor: float32 [1, 2, 1920, 768], P(None, 'tensor', 'dp'), may hold values from -0.21875 to 0.21875
- narrow_outer: float32 [1, 2, 1920, 768], P(None, 'tensor', 'dp'), may hold values from -0.06 to 0.06
- bias_inner: float32 [2, 1, 2, 2304], P('group', None, 'tensor', 'dp'), may hold values from -3 to 3
- bias_first: float32 [2, 1, 2, 2304], P('group', None, 'tensor', 'dp'), may hold values from -19.00703 to 19.00703
- bias_second: float32 [2, 1, 2, 2304], P('group', None, 'tensor', 'dp'), may hold values from 0.8192 to 8.192
- bias_anchor: float32 [1, 2, 2304], P(None, 'tensor', 'dp'), may hold values from -3 to 3
- bias_outer: float32 [1, 2, 2304], P(None, 'tensor', 'dp'), may hold values from -0.06 to 0.06
- norms_inner: float32 [2, 1, 6, 768], P('group', None, None, ('dp', 'tensor')), may hold values from 0.5 to 1.5
- norms_first: float32 [2, 1, 6, 768], P('group', None, None, ('dp', 'tensor')), may hold values from -19.00703 to 19.00703
- norms_second: float32 [2, 1, 6, 768], P('group', None, None, ('dp', 'tensor')), may hold values from 0.8192 to 8.192
- norms_anchor: float32 [1, 6, 768], P(None, None, ('dp', 'tensor')), may hold values from 0.5 to 1.5
- norms_outer: float32 [1, 6, 768], P(None, None, ('dp', 'tensor')), may hold values from -0.06 to 0.06
Outputs:
- layer_out: float32 [2, 16, 512, 768], P(None, ('group', 'dp'), 'tensor')
- input_grad: float32 [2, 16, 512, 768], P(None, ('group', 'dp'), 'tensor')
- wide_grad: float32 [2, 1, 768, 2, 2688], P('group', None, 'dp', 'tensor')
- wide_first_new: float32 [2, 1, 768, 2, 2688], P('group', None, 'dp', 'tensor')
- wide_second_new: float32 [2, 1, 768, 2, 2688], P('group', None, 'dp', 'tensor')
- wide_mean_diff: float32 [1, 768, 2, 2688], P(None, 'dp', 'tensor')
- wide_outer_new: float32 [1, 768, 2, 2688], P(None, 'dp', 'tensor')
- wide_anchor_new: float32 [1, 768, 2, 2688], P(None, 'dp', 'tensor')
- narrow_grad: float32 [2, 1, 2, 1920, 768], P('group', None, 'tensor', 'dp')
- narrow_first_new: float32 [2, 1, 2, 1920, 768], P('group', None, 'tensor', 'dp')
- narrow_second_new: float32 [2, 1, 2, 1920, 768], P('group', None, 'tensor', 'dp')
- narrow_mean_diff: float32 [1, 2, 1920, 768], P(None, 'tensor', 'dp')
- narrow_outer_new: float32 [1, 2, 1920, 768], P(None, 'tensor', 'dp')
- narrow_anchor_new: float32 [1, 2, 1920, 768], P(None, 'tensor', 'dp')
- bias_grad: float32 [2, 1, 2, 2304], P('group', None, 'tensor', 'dp')
- bias_first_new: float32 [2, 1, 2, 2304], P('group', None, 'tensor', 'dp')
- bias_second_new: float32 [2, 1, 2, 2304], P('group', None, 'tensor', 'dp')
- bias_mean_diff: float32 [1, 2, 2304], P(None, 'tensor', 'dp')
- bias_outer_new: float32 [1, 2, 2304], P(None, 'tensor', 'dp')
- bias_anchor_new: float32 [1, 2, 2304], P(None, 'tensor', 'dp')
- norms_grad: float32 [2, 1, 6, 768], P('group', None, None, ('dp', 'tensor'))
- norms_first_new: float32 [2, 1, 6, 768], P('group', None, None, ('dp', 'tensor'))
- norms_second_new: float32 [2, 1, 6, 768], P('group', None, None, ('dp', 'tensor'))
- norms_mean_diff: float32 [1, 6, 768], P(None, None, ('dp', 'tensor'))
- norms_outer_new: float32 [1, 6, 768], P(None, None, ('dp', 'tensor'))
- norms_anchor_new: float32 [1, 6, 768], P(None, None, ('dp', 'tensor'))
The draws below stay inside these ranges and needn't reach their ends.
Inputs may be any that keep to these rules, and one draw needn't show every extreme that they name: `lengths`: slot 0 of every micro-batch is full. `global_blocks`: two different blocks per sequence, both holding real tokens. `rand_blocks`: for each block row and head, three different blocks, none within one block of the row and none of the sequence's global blocks.
All inputs are finite; a program needn't handle non-finite values.
Results may differ from the reference program's by a relative error of at most 0.0095.
The reference program's roundings to bfloat16 on the way count: a program that leaves them out, or rounds other values in their place, can miss the bound.
Values may be sent and summed in bfloat16 or wider, within the bound.
A program may use at most 192 MiB of HBM per device.

```python
import math
import jax
import jax.numpy as jnp
from jax import lax

D = 768
HEADS = 12
FF = 3072
HEAD_DIM = 64
BLOCK = 64
LAYERS = 1
MICRO = 2
SEQ = 512
BLOCKS = 8
SLOTS = 16
DT = 384
FT = 1536
N_GROUP = 2
N_DP = 8
N_TENSOR = 2


def shared_draw(key):
    lengths_all = jax.random.randint(jax.random.fold_in(key, 101), (MICRO, SLOTS), SEQ // 4, SEQ + 1, dtype=jnp.int32)
    lengths_all = lengths_all.at[:, 0].set(SEQ)
    used_blocks = (lengths_all + BLOCK - 1) // BLOCK
    first_pick = jax.random.randint(jax.random.fold_in(key, 102), (MICRO, SLOTS), 0, 1 << 20, dtype=jnp.int32) % used_blocks
    offset_pick = jax.random.randint(jax.random.fold_in(key, 103), (MICRO, SLOTS), 0, 1 << 20, dtype=jnp.int32) % (used_blocks - 1)
    second_pick = (first_pick + 1 + offset_pick) % used_blocks
    global_pair = jnp.stack([first_pick, second_pick], axis=-1)
    block_ids = jnp.arange(BLOCKS, dtype=jnp.int32)
    scores_int = jax.random.randint(jax.random.fold_in(key, 104), (MICRO, SLOTS, BLOCKS, HEADS, BLOCKS), 0, 1 << 20, dtype=jnp.int32)
    scores_int = scores_int * BLOCKS + block_ids
    nearby = jnp.abs(block_ids[:, None] - block_ids[None, :]) <= 1
    global_hit = jnp.any(block_ids[None, None, :, None] == global_pair[:, :, None, :], axis=3)
    banned = nearby[None, None, :, None, :] | global_hit[:, :, None, None, :]
    scores_int = jnp.where(banned, -1, scores_int)
    picked = lax.top_k(scores_int, 3)[1].astype(jnp.int32)
    return (lengths_all, global_pair, picked)


def draw_lengths(key, part):
    return shared_draw(key)[0]


def draw_global_blocks(key, part):
    return shared_draw(key)[1]


def draw_rand_blocks(key, part):
    return shared_draw(key)[2]


def block_levels(key, extent, shards, smallest, high):
    factor_of = 1.0
    for axis_at, blocks in shards:
        steps = jax.random.uniform(jax.random.fold_in(jax.random.fold_in(key, 6), axis_at), (blocks,), jnp.float32, smallest / len(shards), high / len(shards))
        factor_of = factor_of * jnp.repeat(jnp.exp(steps), extent[axis_at] // blocks).reshape((-1,) + (1,) * (len(extent) - 1 - axis_at))
    return factor_of


def gaussian(own_key, shape, deviation, bound, shards=(), kind=jnp.bfloat16):
    level = block_levels(own_key, shape, shards, -0.22, 0.18) if shards else 1.0
    values = jax.random.normal(own_key, shape, jnp.float32) * deviation * level
    return jnp.minimum(jnp.maximum(values, -bound), bound).astype(kind)


def setup_inputs(seed: int = 0) -> dict:
    key_list = jax.random.split(jax.random.key(seed), 27)
    layer_input = gaussian(key_list[0], (MICRO, SLOTS, SEQ, D), 1.0, 6.0, ((1, 16), (2, 2)))
    out_cotangent = gaussian(key_list[1], (MICRO, SLOTS, SEQ, D), 1.0, 6.0, ((1, 16), (2, 2)))
    lengths = draw_lengths(jax.random.fold_in(key_list[26], 71), 0)
    global_blocks = draw_global_blocks(jax.random.fold_in(key_list[26], 71), 0)
    rand_blocks = draw_rand_blocks(jax.random.fold_in(key_list[26], 71), 0)
    inner_steps = jax.random.randint(key_list[5], (N_GROUP,), 1, 21).astype(jnp.int32)
    wide_inner = gaussian(key_list[6], (N_GROUP, LAYERS, D, N_TENSOR, 3 * DT + FT), D ** -0.5, 0.21875, ((0, 2), (2, 8), (3, 2)), jnp.float32)
    wide_first = gaussian(key_list[7], (N_GROUP, LAYERS, D, N_TENSOR, 3 * DT + FT), (0.035 * (MICRO * N_DP * SEQ) ** 0.5), 19.00703, ((0, 2), (2, 8), (3, 2)), jnp.float32)
    wide_second = jnp.clip(jnp.exp(math.log(8.192) - 2.3025852 * jax.random.uniform(key_list[8], (N_GROUP, LAYERS, D, N_TENSOR, 3 * DT + FT), jnp.float32) ** block_levels(key_list[8], (N_GROUP, LAYERS, D, N_TENSOR, 3 * DT + FT), ((0, 2), (2, 8), (3, 2)), -0.2, 0.2)), 0.8192, 8.192)
    wide_anchor = gaussian(key_list[9], (LAYERS, D, N_TENSOR, 3 * DT + FT), D ** -0.5, 0.21875, ((1, 8), (2, 2)), jnp.float32)
    wide_outer = gaussian(key_list[10], (LAYERS, D, N_TENSOR, 3 * DT + FT), 0.01, 0.06, ((1, 8), (2, 2)), jnp.float32)
    narrow_inner = gaussian(key_list[11], (N_GROUP, LAYERS, N_TENSOR, DT + FT, D), (FF // 4) ** -0.5, 0.21875, ((0, 2), (2, 2), (3, 8)), jnp.float32)
    narrow_first = gaussian(key_list[12], (N_GROUP, LAYERS, N_TENSOR, DT + FT, D), (0.035 * (MICRO * N_DP * SEQ) ** 0.5), 19.00703, ((0, 2), (2, 2), (3, 8)), jnp.float32)
    narrow_second = jnp.clip(jnp.exp(math.log(8.192) - 2.3025852 * jax.random.uniform(key_list[13], (N_GROUP, LAYERS, N_TENSOR, DT + FT, D), jnp.float32) ** block_levels(key_list[13], (N_GROUP, LAYERS, N_TENSOR, DT + FT, D), ((0, 2), (2, 2), (3, 8)), -0.2, 0.2)), 0.8192, 8.192)
    narrow_anchor = gaussian(key_list[14], (LAYERS, N_TENSOR, DT + FT, D), (FF // 4) ** -0.5, 0.21875, ((1, 2), (2, 8)), jnp.float32)
    narrow_outer = gaussian(key_list[15], (LAYERS, N_TENSOR, DT + FT, D), 0.01, 0.06, ((1, 2), (2, 8)), jnp.float32)
    bias_inner = gaussian(key_list[16], (N_GROUP, LAYERS, N_TENSOR, 2 * DT + FT), 0.5, 3.0, ((0, 2), (2, 2), (3, 8)), jnp.float32)
    bias_first = gaussian(key_list[17], (N_GROUP, LAYERS, N_TENSOR, 2 * DT + FT), (0.035 * (MICRO * N_DP * SEQ) ** 0.5), 19.00703, ((0, 2), (2, 2), (3, 8)), jnp.float32)
    bias_second = jnp.clip(jnp.exp(math.log(8.192) - 2.3025852 * jax.random.uniform(key_list[18], (N_GROUP, LAYERS, N_TENSOR, 2 * DT + FT), jnp.float32) ** block_levels(key_list[18], (N_GROUP, LAYERS, N_TENSOR, 2 * DT + FT), ((0, 2), (2, 2), (3, 8)), -0.2, 0.2)), 0.8192, 8.192)
    bias_anchor = gaussian(key_list[19], (LAYERS, N_TENSOR, 2 * DT + FT), 0.5, 3.0, ((1, 2), (2, 8)), jnp.float32)
    bias_outer = gaussian(key_list[20], (LAYERS, N_TENSOR, 2 * DT + FT), 0.01, 0.06, ((1, 2), (2, 8)), jnp.float32)
    norms_inner = jnp.clip(0.5 + 1.0 * jax.random.uniform(key_list[21], (N_GROUP, LAYERS, 6, D), jnp.float32) ** block_levels(key_list[21], (N_GROUP, LAYERS, 6, D), ((0, 2), (3, 16)), -0.2, 0.2), 0.5, 1.5)
    norms_first = gaussian(key_list[22], (N_GROUP, LAYERS, 6, D), (0.035 * (MICRO * N_DP * SEQ) ** 0.5), 19.00703, ((0, 2), (3, 16)), jnp.float32)
    norms_second = jnp.clip(jnp.exp(math.log(8.192) - 2.3025852 * jax.random.uniform(key_list[23], (N_GROUP, LAYERS, 6, D), jnp.float32) ** block_levels(key_list[23], (N_GROUP, LAYERS, 6, D), ((0, 2), (3, 16)), -0.2, 0.2)), 0.8192, 8.192)
    norms_anchor = jnp.clip(0.5 + 1.0 * jax.random.uniform(key_list[24], (LAYERS, 6, D), jnp.float32) ** block_levels(key_list[24], (LAYERS, 6, D), ((2, 16),), -0.2, 0.2), 0.5, 1.5)
    norms_outer = gaussian(key_list[25], (LAYERS, 6, D), 0.01, 0.06, ((2, 16),), jnp.float32)
    return dict(layer_input=layer_input, out_cotangent=out_cotangent, lengths=lengths, global_blocks=global_blocks, rand_blocks=rand_blocks, inner_steps=inner_steps, wide_inner=wide_inner, wide_first=wide_first, wide_second=wide_second, wide_anchor=wide_anchor, wide_outer=wide_outer, narrow_inner=narrow_inner, narrow_first=narrow_first, narrow_second=narrow_second, narrow_anchor=narrow_anchor, narrow_outer=narrow_outer, bias_inner=bias_inner, bias_first=bias_first, bias_second=bias_second, bias_anchor=bias_anchor, bias_outer=bias_outer, norms_inner=norms_inner, norms_first=norms_first, norms_second=norms_second, norms_anchor=norms_anchor, norms_outer=norms_outer)


BETA_ONE = 0.9
BETA_TWO = 0.99
ADAM_EPS = 1e-08
LEARN_RATE = 0.04
DECAY_RATE = 0.1
OUTER_BETA = 0.9
OUTER_RATE = 0.7
NORM_EPS = 1e-06
MASKED = -1e+30

@jax.custom_vjp
def low(v):
    return lax.optimization_barrier(v.astype(jnp.bfloat16)).astype(jnp.float32)

@jax.custom_vjp
def low_back(v):
    return v

def low_keep(v):
    return (low(v), None)

def low_pass(kept, grad):
    return (grad,)

def back_keep(v):
    return (v, None)

def back_low(kept, grad):
    return (low(grad),)
low.defvjp(low_keep, low_pass)
low_back.defvjp(back_keep, back_low)

def round_both(value):
    return low_back(low(value))

def product(left, right):
    return jnp.dot(left, right, precision=lax.Precision.HIGHEST, preferred_element_type=jnp.float32)

def layer_norm(value, gain, shift):
    average = lax.optimization_barrier(jnp.mean(value, axis=-1, keepdims=True))
    centred = value - average
    spread = lax.optimization_barrier(jnp.mean(centred * centred, axis=-1, keepdims=True))
    return centred * lax.rsqrt(spread + NORM_EPS) * gain + shift

def block_mask(global_pair, random_rows):
    block_ids = jnp.arange(BLOCKS, dtype=jnp.int32)
    nearby = jnp.abs(block_ids[:, None] - block_ids[None, :]) <= 1
    global_hit = jnp.any(block_ids[:, None] == global_pair[None, :].astype(jnp.int32), axis=1)
    allowed_base = nearby | global_hit[None, :] | global_hit[:, None]
    chosen = jnp.any(jnp.transpose(random_rows.astype(jnp.int32), (1, 0, 2))[:, :, None, :] == block_ids[None, None, :, None], axis=3)
    return allowed_base[None] | chosen

def attend(queries, keys_all, values_all, blocks_ok, length):
    query_rows = min(SEQ, 512)
    block_count = SEQ // query_rows
    per_rows = query_rows // BLOCK
    scaling = HEAD_DIM ** (-0.5)
    key_ok = jnp.arange(SEQ, dtype=jnp.int32) < length
    mask_parts = jnp.transpose(blocks_ok.reshape(HEADS, block_count, per_rows, BLOCKS), (1, 0, 2, 3))
    query_parts = queries.reshape(block_count, query_rows, HEADS, HEAD_DIM)

    def per_block(operands):
        query_part, mask_part = operands
        allowed = jnp.repeat(jnp.repeat(mask_part, BLOCK, axis=1), BLOCK, axis=2) & key_ok[None, None, :]
        raw_scores = jnp.einsum('qhd,khd->hqk', query_part, keys_all, precision=lax.Precision.HIGHEST) * scaling
        scores = low_back(raw_scores)
        masked = jnp.where(allowed, scores, MASKED)
        highest = lax.optimization_barrier(jnp.max(masked, axis=2, keepdims=True))
        weights_exp = jnp.exp(masked - highest)
        prob_rows = weights_exp / lax.optimization_barrier(jnp.sum(weights_exp, axis=2, keepdims=True))
        return jnp.einsum('hqk,khd->qhd', low(prob_rows), values_all, precision=lax.Precision.HIGHEST)
    outputs = lax.map(jax.checkpoint(per_block), (query_parts, mask_parts))
    return outputs.reshape(SEQ, HEADS * HEAD_DIM)

def forward(params, source, blocks_ok, length):
    wide_all, narrow_all, bias_all, norms_all = params
    hidden = source
    for layer_index in range(LAYERS):
        wide_low = low(wide_all[layer_index])
        narrow_low = low(narrow_all[layer_index])
        bias_low = low(bias_all[layer_index])
        row_low = low(norms_all[layer_index])
        w_query = wide_low[:, :, :DT].reshape(D, D)
        w_key = wide_low[:, :, DT:2 * DT].reshape(D, D)
        w_value = wide_low[:, :, 2 * DT:3 * DT].reshape(D, D)
        w_up = wide_low[:, :, 3 * DT:].reshape(D, FF)
        w_out = narrow_low[:, :DT, :].reshape(D, D)
        w_down = narrow_low[:, DT:, :].reshape(FF, D)
        b_query = bias_low[:, :DT].reshape(D)
        b_value = bias_low[:, DT:2 * DT].reshape(D)
        b_up = bias_low[:, 2 * DT:].reshape(FF)
        inputs_one = low(hidden)
        queries = round_both(product(inputs_one, w_query) + b_query)
        keys_all = round_both(product(inputs_one, w_key))
        values_all = round_both(product(inputs_one, w_value) + b_value)
        mixed = round_both(attend(queries.reshape(SEQ, HEADS, HEAD_DIM), keys_all.reshape(SEQ, HEADS, HEAD_DIM), values_all.reshape(SEQ, HEADS, HEAD_DIM), blocks_ok, length))
        branch = low_back(product(mixed, w_out))
        first_out = layer_norm(hidden + branch + row_low[0], row_low[2], row_low[3])
        inputs_two = low(first_out)
        inner_pre = low_back(product(inputs_two, w_up) + b_up)
        gelu_out = low(jax.nn.gelu(inner_pre, approximate=True))
        branch_two = low_back(product(gelu_out, w_down))
        hidden = layer_norm(first_out + branch_two + row_low[1], row_low[4], row_low[5])
    return hidden

def adam_step(weight, gradient, first, second, count):
    first_new = BETA_ONE * first + (1.0 - BETA_ONE) * gradient
    second_new = BETA_TWO * second + (1.0 - BETA_TWO) * gradient * gradient
    first_hat = first_new / (1.0 - BETA_ONE ** count)
    second_hat = second_new / (1.0 - BETA_TWO ** count)
    weight_new = weight - LEARN_RATE * (first_hat / (jnp.sqrt(second_hat) + ADAM_EPS) + DECAY_RATE * weight)
    return (weight_new, first_new, second_new)

def reference(layer_input, out_cotangent, lengths, global_blocks, rand_blocks, inner_steps, wide_inner, wide_first, wide_second, wide_anchor, wide_outer, narrow_inner, narrow_first, narrow_second, narrow_anchor, narrow_outer, bias_inner, bias_first, bias_second, bias_anchor, bias_outer, norms_inner, norms_first, norms_second, norms_anchor, norms_outer):
    inners = (wide_inner, narrow_inner, bias_inner, norms_inner)
    firsts = (wide_first, narrow_first, bias_first, norms_first)
    seconds = (wide_second, narrow_second, bias_second, norms_second)
    anchors = (wide_anchor, narrow_anchor, bias_anchor, norms_anchor)
    outers = (wide_outer, narrow_outer, bias_outer, norms_outer)
    out_parts = []
    grad_parts = []
    group_grads = []
    group_firsts = []
    group_seconds = []
    group_weights = []
    for group_index in range(N_GROUP):
        params = tuple((arr[group_index] for arr in inners))
        first_slot = group_index * N_DP
        last_slot = first_slot + N_DP
        sources = layer_input[:, first_slot:last_slot].astype(jnp.float32).reshape(MICRO * N_DP, SEQ, D)
        cot_rows = out_cotangent[:, first_slot:last_slot].astype(jnp.float32).reshape(MICRO * N_DP, SEQ, D)
        length_rows = lengths[:, first_slot:last_slot].reshape(MICRO * N_DP).astype(jnp.int32)
        global_rows = global_blocks[:, first_slot:last_slot].reshape(MICRO * N_DP, 2).astype(jnp.int32)
        random_rows = rand_blocks[:, first_slot:last_slot].reshape(MICRO * N_DP, BLOCKS, HEADS, 3).astype(jnp.int32)
        zeros_init = tuple((jnp.zeros(arr.shape, jnp.float32) for arr in params))

        def per_sequence(running, operands):
            source, weight_cot, length, global_pair, random_sel = operands
            blocks_ok = block_mask(global_pair, random_sel)

            def apply_layers(param_set, source_rows):
                return forward(param_set, source_rows, blocks_ok, length)
            output, pull = jax.vjp(apply_layers, params, source)
            keep_rows = (jnp.arange(SEQ, dtype=jnp.int32) < length).astype(jnp.float32)[:, None]
            grad_params, grad_source = pull(weight_cot * keep_rows)
            running = tuple((left + right for left, right in zip(running, grad_params)))
            return (running, (output, grad_source))
        summed, (outputs, grad_sources) = lax.scan(per_sequence, zeros_init, (sources, cot_rows, length_rows, global_rows, random_rows))
        out_parts.append(outputs.reshape(MICRO, N_DP, SEQ, D))
        grad_parts.append(grad_sources.reshape(MICRO, N_DP, SEQ, D))
        count = inner_steps[group_index].astype(jnp.float32)
        updated = [adam_step(params[kind], summed[kind], firsts[kind][group_index], seconds[kind][group_index], count) for kind in range(4)]
        group_grads.append(summed)
        group_weights.append(tuple((item[0] for item in updated)))
        group_firsts.append(tuple((item[1] for item in updated)))
        group_seconds.append(tuple((item[2] for item in updated)))
    layer_out = jnp.concatenate(out_parts, axis=1)
    input_grad = jnp.concatenate(grad_parts, axis=1)
    results = []
    for kind in range(4):
        grad_stack = jnp.stack([group_grads[idx][kind] for idx in range(N_GROUP)])
        first_stack = jnp.stack([group_firsts[idx][kind] for idx in range(N_GROUP)])
        second_stack = jnp.stack([group_seconds[idx][kind] for idx in range(N_GROUP)])
        diff_total = jnp.zeros(anchors[kind].shape, jnp.float32)
        for idx in range(N_GROUP):
            diff_total = diff_total + (anchors[kind] - group_weights[idx][kind])
        mean_diff = diff_total / N_GROUP
        outer_new = OUTER_BETA * outers[kind] + mean_diff
        anchor_new = anchors[kind] - OUTER_RATE * (mean_diff + OUTER_BETA * outer_new)
        results.append((grad_stack, first_stack, second_stack, mean_diff, outer_new, anchor_new))
    return (layer_out, input_grad, results[0][0], results[0][1], results[0][2], results[0][3], results[0][4], results[0][5], results[1][0], results[1][1], results[1][2], results[1][3], results[1][4], results[1][5], results[2][0], results[2][1], results[2][2], results[2][3], results[2][4], results[2][5], results[3][0], results[3][1], results[3][2], results[3][3], results[3][4], results[3][5])
```

```python
import jax
import jax.numpy as jnp
from jax import lax
from jax.experimental import pallas as pl
from jax.experimental.pallas import tpu as pltpu
from jax.sharding import PartitionSpec as P

BETA_ONE = 0.9
BETA_TWO = 0.99
ADAM_EPS = 1e-08
LEARN_RATE = 0.04
DECAY_RATE = 0.1
OUTER_BETA = 0.9
OUTER_RATE = 0.7
NORM_EPS = 1e-06
MASKED = -1e30

MESH = pl.DeviceIdType.MESH
ZS = 4
F32, BF16 = jnp.float32, jnp.bfloat16


def place():
    d = lax.axis_index("dp")
    return d // 2, lax.rem(d, 2)


def neighbours():
    g, t = lax.axis_index("group"), lax.axis_index("tensor")
    z, x = place()
    return dict(
        x=(g, z * 2 + (1 - x), t),
        up=(g, (z + 1) * 2 + x, t),
        down=(g, (z - 1) * 2 + x, t),
        core=(g, z * 2 + x, 1 - t),
        group=(1 - g, z * 2 + x, t),
    )


def entry_barrier():
    z, _ = place()
    near = neighbours()
    bar = pltpu.get_barrier_semaphore()

    def greet(name):
        pl.semaphore_signal(bar, inc=1, device_id=near[name], device_id_type=MESH)

    for name in ("x", "core", "group"):
        greet(name)
    pl.when(z < ZS - 1)(lambda: greet("up"))
    pl.when(z > 0)(lambda: greet("down"))
    pl.semaphore_wait(bar, 3 + (z + 2) // 3 + (ZS + 1 - z) // 3)


WAYS = {"x": 0, "up": 1, "down": 2}


class Gather:
    def __init__(self, view, ssem, rsem):
        self.view, self.ssem, self.rsem = view, ssem, rsem
        self.near = neighbours()
        self.z, self.x = place()

    def copy(self, g, zsrc, xsrc, way):
        ref = self.view(g, zsrc * 2 + xsrc)
        return pltpu.make_async_remote_copy(
            src_ref=ref,
            dst_ref=ref,
            send_sem=self.ssem.at[g, zsrc, WAYS[way]],
            recv_sem=self.rsem.at[g, zsrc * 2 + xsrc],
            device_id=self.near[way],
            device_id_type=MESH,
        )

    def own(self, g, only=None):
        z, x = self.z, self.x
        ok = (z >= 0) if only is None else only(z)
        pl.when(ok)(lambda: self.copy(g, z, x, "x").start())
        pl.when(ok & (z < ZS - 1))(lambda: self.copy(g, z, x, "up").start())
        pl.when(ok & (z > 0))(lambda: self.copy(g, z, x, "down").start())

    def relay(self, g, k, only=None):
        z, x = self.z, self.x
        for way, src in (("up", z - k), ("down", z + k)):
            ok = (src >= 0) if way == "up" else (src < ZS)
            if only is not None:
                ok = ok & only(src)
            more = (z < ZS - 1) if way == "up" else (z > 0)

            @pl.when(ok)
            def _():
                self.copy(g, src, x, way).wait_recv()
                self.copy(g, src, x, "x").start()
                pl.when(more)(lambda: self.copy(g, src, x, way).start())

    def across(self, g, srcs=range(ZS)):
        for zsrc in srcs:
            self.copy(g, zsrc, 1 - self.x, "x").wait_recv()

    def drain(self, g, srcs=range(ZS)):
        z, x = self.z, self.x
        for zsrc in srcs:
            self.copy(g, zsrc, x, "x").wait_send()
            pl.when((zsrc <= z) & (z < ZS - 1))(lambda: self.copy(g, zsrc, x, "up").wait_send())
            pl.when((zsrc >= z) & (z > 0))(lambda: self.copy(g, zsrc, x, "down").wait_send())


def far_order(z, k):
    if k == 0:
        return 3 * (1 - z // 2)
    if k == 1:
        return lax.rem(2 + 3 * z, 5)
    if k == 2:
        return 1 + lax.rem(z, 2)
    return z


class Scatter:
    def __init__(self, source, xbuf, zbuf, xs, xr, zs, zr):
        self.source, self.xbuf, self.zbuf = source, xbuf, zbuf
        self.xs, self.xr, self.zs, self.zr = xs, xr, zs, zr
        self.near = neighbours()
        self.z, self.x = place()

    def xcopy(self, g, row):
        return pltpu.make_async_remote_copy(
            src_ref=self.source(g, row * 2 + (1 - self.x)),
            dst_ref=self.xbuf(g, row),
            send_sem=self.xs.at[g, row],
            recv_sem=self.xr.at[g, row],
            device_id=self.near["x"],
            device_id_type=MESH,
        )

    def zcopy(self, g, row, slot, way):
        return pltpu.make_async_remote_copy(
            src_ref=self.xbuf(g, row),
            dst_ref=self.zbuf(g, slot),
            send_sem=self.zs.at[g, row],
            recv_sem=self.zr.at[g, slot],
            device_id=self.near[way],
            device_id_type=MESH,
        )

    def send(self, g, k, only=None):
        row = far_order(self.z, k)
        ok = (row >= 0) if only is None else only(row)
        pl.when(ok)(lambda: self.xcopy(g, row).start())

    def pass_on(self, g, k, only=None):
        z, x = self.z, self.x
        row = far_order(z, k)
        ok = (row >= 0) if only is None else only(row)

        @pl.when(ok)
        def _():
            self.xcopy(g, row).wait_recv()
            below = z < row
            further = (below & (z > 0)) | ((z > row) & (z < ZS - 1))
            src, buf = self.source(g, row * 2 + x), self.xbuf(g, row)

            @pl.when(further)
            def _():
                self.zcopy(g, row, row, "up").wait_recv()
                buf[...] = (
                    src[...].astype(F32) + buf[...].astype(F32) + self.zbuf(g, row)[...].astype(F32)
                ).astype(BF16)

            @pl.when(jnp.logical_not(further))
            def _():
                buf[...] = (src[...].astype(F32) + buf[...].astype(F32)).astype(BF16)

            pl.when(below & (z + 1 < row))(lambda: self.zcopy(g, row, row, "up").start())
            pl.when(below & (z + 1 == row))(lambda: self.zcopy(g, row, ZS, "up").start())
            pl.when(z > row)(lambda: self.zcopy(g, row, row, "down").start())

    def finish(self, g, result, only=None):
        z, x = self.z, self.x
        ok = (z >= 0) if only is None else only(z)

        @pl.when(ok)
        def _():
            self.xcopy(g, z).wait_recv()
            out = result(g)
            out[...] = self.source(g, z * 2 + x)[...].astype(F32) + self.xbuf(g, z)[...].astype(F32)

            @pl.when(z < ZS - 1)
            def _():
                self.zcopy(g, z, z, "down").wait_recv()
                out[...] += self.zbuf(g, z)[...].astype(F32)

            @pl.when(z > 0)
            def _():
                self.zcopy(g, z, ZS, "up").wait_recv()
                out[...] += self.zbuf(g, ZS)[...].astype(F32)

    def drain(self, g, k, only=None):
        row = far_order(self.z, k)
        ok = (row >= 0) if only is None else only(row)

        @pl.when(ok)
        def _():
            self.xcopy(g, row).wait_send()
            if k < 3:
                self.zcopy(g, row, row, "up").wait_send()


VMEM_SPEC = pl.BlockSpec(memory_space=pltpu.VMEM)
DMA = pltpu.SemaphoreType.DMA
BIG_VMEM = 56 * 1024 * 1024


def first_row(row):
    return row == 0


def other_rows(row):
    return row > 0


def shard_view(wide, narrow, split):
    rows, cols = wide.shape[0] // 8, wide.shape[1]
    deep = narrow.shape[0] // 8

    def view(g, shard):
        if g == 2:
            return narrow.at[pl.ds(pl.multiple_of(shard * deep, deep), deep)]
        at = pl.ds(pl.multiple_of(shard * rows, rows), rows)
        return wide.at[at, pl.ds(0, split)] if g == 0 else wide.at[at, pl.ds(split, cols - split)]

    return view


def gather_kernel(split, wide_own, narrow_own, wide, narrow, ssem, rsem):
    z, x = place()
    shard = z * 2 + x
    rows, deep = wide_own.shape[0], narrow_own.shape[0]
    wide[pl.ds(pl.multiple_of(shard * rows, rows), rows), :] = wide_own[...].astype(BF16)
    narrow[pl.ds(pl.multiple_of(shard * deep, deep), deep), :] = narrow_own[...].astype(BF16)
    entry_barrier()
    work = Gather(shard_view(wide, narrow, split), ssem, rsem)
    order = (0, 2, 1)
    work.own(0)
    for at, g in enumerate(order):
        work.relay(g, 1)
        if at < 2:
            work.own(order[at + 1])
        work.relay(g, 2)
        work.relay(g, 3)
    for g in range(3):
        work.across(g)
    for g in range(3):
        work.drain(g)


def gather_weights(wide_own, narrow_own, split):
    return pl.pallas_call(
        lambda *refs: gather_kernel(split, *refs),
        out_shape=(
            jax.ShapeDtypeStruct((8 * wide_own.shape[0], wide_own.shape[1]), BF16),
            jax.ShapeDtypeStruct((8 * narrow_own.shape[0], narrow_own.shape[1]), BF16),
        ),
        in_specs=[VMEM_SPEC] * 2,
        out_specs=(VMEM_SPEC,) * 2,
        scratch_shapes=[DMA((3, 4, 3)), DMA((3, 8))],
        compiler_params=pltpu.CompilerParams(
            collective_id=1, has_side_effects=True, vmem_limit_bytes=BIG_VMEM
        ),
        name="gather_weights",
    )(wide_own, narrow_own)


def scatter_kernel(split, wide, narrow, wide_out, narrow_out, xw, xn, zw, zn, xs, xr, zs, zr):
    entry_barrier()
    cols = wide.shape[1]

    def half(g):
        return pl.ds(0, split) if g == 0 else pl.ds(split, cols - split)

    work = Scatter(
        shard_view(wide, narrow, split),
        lambda g, row: xn.at[row] if g == 2 else xw.at[row, :, half(g)],
        lambda g, row: zn.at[row] if g == 2 else zw.at[row, :, half(g)],
        xs,
        xr,
        zs,
        zr,
    )

    def result(g):
        return narrow_out if g == 2 else wide_out.at[:, half(g)]

    for g in (2, 1, 0):
        for k in range(4):
            work.send(g, k)
    for g in (2, 1, 0):
        for k in range(3):
            work.pass_on(g, k)
        work.finish(g, result)
    for g in (2, 1, 0):
        for k in range(4):
            work.drain(g, k)


def scatter_grads(wide, narrow, split):
    rows, cols = wide.shape[0] // 8, wide.shape[1]
    deep, width = narrow.shape[0] // 8, narrow.shape[1]
    return pl.pallas_call(
        lambda *refs: scatter_kernel(split, *refs),
        out_shape=(
            jax.ShapeDtypeStruct((rows, cols), F32),
            jax.ShapeDtypeStruct((deep, width), F32),
        ),
        in_specs=[VMEM_SPEC] * 2,
        out_specs=(VMEM_SPEC,) * 2,
        scratch_shapes=[
            pltpu.VMEM((ZS, rows, cols), BF16),
            pltpu.VMEM((ZS, deep, width), BF16),
            pltpu.VMEM((ZS + 1, rows, cols), BF16),
            pltpu.VMEM((ZS + 1, deep, width), BF16),
            DMA((3, ZS)),
            DMA((3, ZS)),
            DMA((3, ZS)),
            DMA((3, ZS + 1)),
        ],
        compiler_params=pltpu.CompilerParams(
            collective_id=2, has_side_effects=True, vmem_limit_bytes=BIG_VMEM
        ),
        name="scatter_grads",
    )(wide, narrow)


def gelu_tanh(values):
    return jax.nn.gelu(values, approximate=True)


def norm_stats(values):
    average = jnp.mean(values, axis=-1, keepdims=True)
    centred = values - average
    spread = jnp.mean(centred * centred, axis=-1, keepdims=True)
    scaling = lax.rsqrt(spread + NORM_EPS)
    return (centred * scaling, scaling)


def norm_back(grad_rows, normed, scaling, gain):
    scaled = grad_rows * gain
    return scaling * (
        scaled
        - jnp.mean(scaled, axis=-1, keepdims=True)
        - normed * jnp.mean(scaled * normed, axis=-1, keepdims=True)
    )


def rows_forward(values):
    return lax.all_gather(values, "tensor", axis=0, tiled=True)


def sum_forward(values):
    return lax.psum_scatter(values, "tensor", scatter_dimension=0, tiled=True)


def rows_backward(values):
    return lax.all_gather(values, "tensor", axis=0, tiled=True)


def sum_backward(values):
    return lax.psum_scatter(values, "tensor", scatter_dimension=0, tiled=True)


def block_mask(global_pair, random_rows, block_total):
    block_ids = jnp.arange(block_total, dtype=jnp.int32)
    nearby = jnp.abs(block_ids[:, None] - block_ids[None, :]) <= 1
    global_hit = jnp.any(block_ids[:, None] == global_pair[None, :], axis=1)
    allowed_base = nearby | global_hit[None, :] | global_hit[:, None]
    chosen = jnp.any(
        jnp.transpose(random_rows, (1, 0, 2))[:, :, None, :] == block_ids[None, None, :, None],
        axis=3,
    )
    return allowed_base[None] | chosen


def split_blocks(blocks_ok, seq_len, block_len):
    heads_dev = blocks_ok.shape[0]
    query_rows = min(seq_len, 512)
    block_count = seq_len // query_rows
    per_rows = query_rows // block_len
    mask_parts = jnp.transpose(
        blocks_ok.reshape(heads_dev, block_count, per_rows, -1), (1, 0, 2, 3)
    )
    return (mask_parts, query_rows, block_count)


def attend_forward(queries, keys_all, values_all, blocks_ok, key_ok, block_len):
    seq_len, heads_dev, head_width = queries.shape
    scaling = head_width ** (-0.5)
    mask_parts, query_rows, block_count = split_blocks(blocks_ok, seq_len, block_len)
    query_parts = queries.reshape(block_count, query_rows, heads_dev, head_width)

    def per_block(operands):
        query_part, mask_part = operands
        allowed = (
            jnp.repeat(jnp.repeat(mask_part, block_len, axis=1), block_len, axis=2)
            & key_ok[None, None, :]
        )
        scores = (
            jnp.einsum("qhd,khd->hqk", query_part, keys_all, preferred_element_type=jnp.float32)
            * scaling
        )
        masked = jnp.where(allowed, scores, MASKED)
        highest = jnp.max(masked, axis=2, keepdims=True)
        weights_exp = jnp.exp(masked - highest)
        summed = jnp.sum(weights_exp, axis=2, keepdims=True)
        prob_rows = (weights_exp / summed).astype(jnp.bfloat16)
        outputs = jnp.einsum(
            "hqk,khd->qhd", prob_rows, values_all, preferred_element_type=jnp.float32
        )
        return (outputs, (highest + jnp.log(summed))[:, :, 0])

    outputs, log_totals = lax.map(per_block, (query_parts, mask_parts))
    return (outputs.reshape(seq_len, heads_dev * head_width), log_totals)


def attend_backward(
    queries, keys_all, values_all, grad_mixed, log_totals, blocks_ok, key_ok, block_len
):
    seq_len, heads_dev, head_width = queries.shape
    scaling = head_width ** (-0.5)
    mask_parts, query_rows, block_count = split_blocks(blocks_ok, seq_len, block_len)
    query_parts = queries.reshape(block_count, query_rows, heads_dev, head_width)
    grad_parts = grad_mixed.reshape(block_count, query_rows, heads_dev, head_width)

    def per_block(running, operands):
        key_total, value_total = running
        query_part, mask_part, grad_part, total_part = operands
        allowed = (
            jnp.repeat(jnp.repeat(mask_part, block_len, axis=1), block_len, axis=2)
            & key_ok[None, None, :]
        )
        scores = (
            jnp.einsum("qhd,khd->hqk", query_part, keys_all, preferred_element_type=jnp.float32)
            * scaling
        )
        prob_rows = jnp.exp(jnp.where(allowed, scores, MASKED) - total_part[:, :, None])
        grad_probs = jnp.einsum(
            "qhd,khd->hqk", grad_part, values_all, preferred_element_type=jnp.float32
        )
        centre = jnp.sum(prob_rows * grad_probs, axis=2, keepdims=True)
        grad_scores = (prob_rows * (grad_probs - centre)).astype(jnp.bfloat16)
        query_grad = (
            jnp.einsum("hqk,khd->qhd", grad_scores, keys_all, preferred_element_type=jnp.float32)
            * scaling
        )
        key_total = (
            key_total
            + jnp.einsum(
                "hqk,qhd->khd", grad_scores, query_part, preferred_element_type=jnp.float32
            )
            * scaling
        )
        value_total = value_total + jnp.einsum(
            "hqk,qhd->khd",
            prob_rows.astype(jnp.bfloat16),
            grad_part,
            preferred_element_type=jnp.float32,
        )
        return ((key_total, value_total), query_grad)

    zeros_init = jnp.zeros(keys_all.shape, jnp.float32)
    (key_grad, value_grad), query_grad = lax.scan(
        per_block, (zeros_init, zeros_init), (query_parts, mask_parts, grad_parts, log_totals)
    )
    flat = heads_dev * head_width
    return (
        query_grad.reshape(seq_len, flat),
        key_grad.reshape(seq_len, flat),
        value_grad.reshape(seq_len, flat),
    )


def adam_step(weight, gradient, first, second, count):
    first_new = BETA_ONE * first + (1.0 - BETA_ONE) * gradient
    second_new = BETA_TWO * second + (1.0 - BETA_TWO) * gradient * gradient
    first_hat = first_new / (1.0 - BETA_ONE**count)
    second_hat = second_new / (1.0 - BETA_TWO**count)
    weight_new = weight - LEARN_RATE * (
        first_hat / (jnp.sqrt(second_hat) + ADAM_EPS) + DECAY_RATE * weight
    )
    return (weight_new, first_new, second_new)


def on_device(
    layer_input,
    out_cotangent,
    lengths,
    global_blocks,
    rand_blocks,
    inner_steps,
    wide_inner,
    wide_first,
    wide_second,
    wide_anchor,
    wide_outer,
    narrow_inner,
    narrow_first,
    narrow_second,
    narrow_anchor,
    narrow_outer,
    bias_inner,
    bias_first,
    bias_second,
    bias_anchor,
    bias_outer,
    norms_inner,
    norms_first,
    norms_second,
    norms_anchor,
    norms_outer,
):
    micro_count = layer_input.shape[0]
    row_count = layer_input.shape[2]
    layers = wide_inner.shape[1]
    tensor_count = lax.axis_size("tensor")
    seq_len = row_count * tensor_count
    block_total = rand_blocks.shape[2]
    block_len = seq_len // block_total
    heads_dev = rand_blocks.shape[3]
    model_width = layer_input.shape[3]
    head_width = model_width // (heads_dev * tensor_count)
    attn_cols = heads_dev * head_width
    own_rows = lax.axis_index("tensor") * row_count + jnp.arange(row_count, dtype=jnp.int32)
    norms_full = lax.all_gather(
        norms_inner[0].astype(jnp.bfloat16), ("dp", "tensor"), axis=2, tiled=True
    ).astype(jnp.float32)
    fast = lax.axis_size("dp") == 8 and wide_inner.shape[2] % 16 == 0 and layers == 1
    if fast:
        gathered = (
            *gather_weights(wide_inner[0, 0, :, 0, :], narrow_inner[0, 0, 0], 3 * attn_cols),
            lax.all_gather(bias_inner[0, 0, 0].astype(jnp.bfloat16), "dp", axis=0, tiled=True),
        )
    outs_rows = []
    grads_rows = []
    collected = []
    collected_rows = []
    for micro_index in range(micro_count):
        if fast:
            weights = [gathered]
        else:
            weights = [
                (
                    lax.all_gather(
                        wide_inner[0, 0, :, 0, :].astype(jnp.bfloat16), "dp", axis=0, tiled=True
                    ),
                    lax.all_gather(
                        narrow_inner[0, 0, 0].astype(jnp.bfloat16), "dp", axis=0, tiled=True
                    ),
                    lax.all_gather(bias_inner[0, 0, 0].astype(jnp.bfloat16), "dp", axis=0, tiled=True),
                )
            ]
        length = lengths[micro_index, 0]
        key_ok = jnp.arange(seq_len, dtype=jnp.int32) < length
        row_ok = (own_rows < length).astype(jnp.float32)[:, None]
        blocks_ok = block_mask(
            global_blocks[micro_index, 0], rand_blocks[micro_index, 0], block_total
        )
        hidden = layer_input[micro_index, 0].astype(jnp.float32)
        layer_index = 0
        w_wide, w_narrow, w_bias = weights[layer_index]
        bias_rows = w_bias.astype(jnp.float32)
        norm_rows = norms_full[layer_index]
        inputs_one = rows_forward(hidden.astype(jnp.bfloat16))
        qkv_bias = jnp.concatenate(
            [
                bias_rows[:attn_cols],
                jnp.zeros((attn_cols,), jnp.float32),
                bias_rows[attn_cols : 2 * attn_cols],
            ]
        )
        qkv = (
            jnp.dot(inputs_one, w_wide[:, : 3 * attn_cols], preferred_element_type=jnp.float32)
            + qkv_bias
        ).astype(jnp.bfloat16)
        queries = qkv[:, :attn_cols].reshape(seq_len, heads_dev, head_width)
        keys_all = qkv[:, attn_cols : 2 * attn_cols].reshape(seq_len, heads_dev, head_width)
        values_all = qkv[:, 2 * attn_cols :].reshape(seq_len, heads_dev, head_width)
        mixed, log_totals = attend_forward(
            queries, keys_all, values_all, blocks_ok, key_ok, block_len
        )
        mixed = mixed.astype(jnp.bfloat16)
        branch = sum_forward(
            jnp.dot(mixed, w_narrow[:attn_cols], preferred_element_type=jnp.float32)
        )
        normed, scaling = norm_stats(hidden + branch + norm_rows[0])
        first_out = normed * norm_rows[2] + norm_rows[3]
        inputs_two = rows_forward(first_out.astype(jnp.bfloat16))
        inner_pre = (
            jnp.dot(inputs_two, w_wide[:, 3 * attn_cols :], preferred_element_type=jnp.float32)
            + bias_rows[2 * attn_cols :]
        )
        gelu_vals, gelu_pull = jax.vjp(gelu_tanh, inner_pre)
        gelu_out = gelu_vals.astype(jnp.bfloat16)
        branch_two = sum_forward(
            jnp.dot(gelu_out, w_narrow[attn_cols:], preferred_element_type=jnp.float32)
        )
        normed_two, scaling_two = norm_stats(first_out + branch_two + norm_rows[1])
        stored = [
            (
                inputs_one,
                queries,
                keys_all,
                values_all,
                mixed,
                log_totals,
                normed,
                scaling,
                inputs_two,
                gelu_pull,
                gelu_out,
                normed_two,
                scaling_two,
            )
        ]
        hidden = normed_two * norm_rows[4] + norm_rows[5]
        outs_rows.append(hidden)
        grad_rows = out_cotangent[micro_index, 0].astype(jnp.float32) * row_ok
        pieces = [None] * layers
        for layer_index in reversed(range(layers)):
            (
                inputs_one,
                queries,
                keys_all,
                values_all,
                mixed,
                log_totals,
                normed,
                scaling,
                inputs_two,
                gelu_pull,
                gelu_out,
                normed_two,
                scaling_two,
            ) = stored[layer_index]
            w_wide, w_narrow, w_bias = weights[layer_index]
            norm_rows = norms_full[layer_index]
            gain_two_grad = jnp.sum(grad_rows * normed_two, axis=0)
            shift_two_grad = jnp.sum(grad_rows, axis=0)
            residual_two = norm_back(grad_rows, normed_two, scaling_two, norm_rows[4])
            down_bias_grad = jnp.sum(residual_two, axis=0)
            full_two = rows_backward(residual_two.astype(jnp.bfloat16))
            down_grad = jnp.einsum(
                "sf,sd->fd", gelu_out, full_two, preferred_element_type=jnp.float32
            )
            gelu_grad = jnp.einsum(
                "sd,fd->sf", full_two, w_narrow[attn_cols:], preferred_element_type=jnp.float32
            )
            inner_grad = gelu_pull(gelu_grad)[0].astype(jnp.bfloat16)
            up_bias_grad = jnp.sum(inner_grad, axis=0, dtype=jnp.float32)
            up_grad = jnp.einsum(
                "sd,sf->df", inputs_two, inner_grad, preferred_element_type=jnp.float32
            )
            first_grad = residual_two + sum_backward(
                jnp.einsum(
                    "sf,df->sd",
                    inner_grad,
                    w_wide[:, 3 * attn_cols :],
                    preferred_element_type=jnp.float32,
                )
            )
            gain_one_grad = jnp.sum(first_grad * normed, axis=0)
            shift_one_grad = jnp.sum(first_grad, axis=0)
            residual_one = norm_back(first_grad, normed, scaling, norm_rows[2])
            out_bias_grad = jnp.sum(residual_one, axis=0)
            full_one = rows_backward(residual_one.astype(jnp.bfloat16))
            out_grad = jnp.einsum("sa,sd->ad", mixed, full_one, preferred_element_type=jnp.float32)
            mixed_grad = jnp.einsum(
                "sd,ad->sa", full_one, w_narrow[:attn_cols], preferred_element_type=jnp.float32
            ).astype(jnp.bfloat16)
            query_grad, key_grad, value_grad = attend_backward(
                queries,
                keys_all,
                values_all,
                mixed_grad.reshape(seq_len, heads_dev, head_width),
                log_totals,
                blocks_ok,
                key_ok,
                block_len,
            )
            qkv_grad = jnp.concatenate([query_grad, key_grad, value_grad], axis=1).astype(
                jnp.bfloat16
            )
            query_bias_grad = jnp.sum(qkv_grad[:, :attn_cols], axis=0, dtype=jnp.float32)
            value_bias_grad = jnp.sum(qkv_grad[:, 2 * attn_cols :], axis=0, dtype=jnp.float32)
            attn_weight_grad = jnp.einsum(
                "sd,sc->dc", inputs_one, qkv_grad, preferred_element_type=jnp.float32
            )
            grad_rows = residual_one + sum_backward(
                jnp.einsum(
                    "sc,dc->sd",
                    qkv_grad,
                    w_wide[:, : 3 * attn_cols],
                    preferred_element_type=jnp.float32,
                )
            )
            pieces[layer_index] = (
                jnp.concatenate([attn_weight_grad, up_grad], axis=1),
                jnp.concatenate([out_grad, down_grad], axis=0),
                jnp.concatenate([query_bias_grad, value_bias_grad, up_bias_grad]),
                jnp.stack(
                    [
                        out_bias_grad,
                        down_bias_grad,
                        gain_one_grad,
                        shift_one_grad,
                        gain_two_grad,
                        shift_two_grad,
                    ]
                ),
            )
        grads_rows.append(grad_rows)
        micro_pieces = (
            jnp.stack([item[0] for item in pieces]),
            jnp.stack([item[1] for item in pieces]),
            jnp.stack([item[2] for item in pieces]),
        )
        collected_rows.append(jnp.stack([item[3] for item in pieces]))
        collected.append(micro_pieces)
    merged = collected[0]
    for extra in collected[1:]:
        merged = jax.tree.map(jnp.add, merged, extra)
    merged_rows = collected_rows[0]
    for extra in collected_rows[1:]:
        merged_rows = merged_rows + extra
    if fast:
        wide_sum, narrow_sum = scatter_grads(
            merged[0][0].astype(BF16), merged[1][0].astype(BF16), 3 * attn_cols
        )
        shards = (wide_sum[None], narrow_sum[None])
    else:
        shards = (
            lax.psum_scatter(merged[0], "dp", scatter_dimension=1, tiled=True),
            lax.psum_scatter(merged[1], "dp", scatter_dimension=1, tiled=True),
        )
    shards = shards + (lax.psum_scatter(merged[2], "dp", scatter_dimension=1, tiled=True),)
    row_shard = lax.psum_scatter(merged_rows, ("dp", "tensor"), scatter_dimension=2, tiled=True)
    grads = (
        shards[0][None, :, :, None, :],
        shards[1][None, :, None],
        shards[2][None, :, None],
        row_shard[None],
    )
    inners = (wide_inner, narrow_inner, bias_inner, norms_inner)
    firsts = (wide_first, narrow_first, bias_first, norms_first)
    seconds = (wide_second, narrow_second, bias_second, norms_second)
    anchors = (wide_anchor, narrow_anchor, bias_anchor, norms_anchor)
    outers = (wide_outer, narrow_outer, bias_outer, norms_outer)
    count = inner_steps[0].astype(jnp.float32)
    updated = [
        adam_step(inners[kind], grads[kind], firsts[kind], seconds[kind], count)
        for kind in range(4)
    ]
    diffs = tuple((anchors[kind] - updated[kind][0][0] for kind in range(4)))
    group_count = lax.axis_size("group")
    if fast and group_count == 2:
        sent = tuple(diff.astype(BF16) for diff in diffs)
        diff_sums = tuple(
            here.astype(F32) + lax.ppermute(here, "group", ((0, 1), (1, 0))).astype(F32)
            for here in sent
        )
    else:
        diff_sums = lax.psum((diffs[0], diffs[1], diffs[2], diffs[3]), "group")
    results = []
    for kind in range(4):
        mean_diff = diff_sums[kind] / group_count
        outer_new = OUTER_BETA * outers[kind] + mean_diff
        anchor_new = anchors[kind] - OUTER_RATE * (mean_diff + OUTER_BETA * outer_new)
        results.append(
            (grads[kind], updated[kind][1], updated[kind][2], mean_diff, outer_new, anchor_new)
        )
    layer_out = jnp.stack(outs_rows)[:, None]
    input_grad = jnp.stack(grads_rows)[:, None]
    return (
        layer_out,
        input_grad,
        results[0][0],
        results[0][1],
        results[0][2],
        results[0][3],
        results[0][4],
        results[0][5],
        results[1][0],
        results[1][1],
        results[1][2],
        results[1][3],
        results[1][4],
        results[1][5],
        results[2][0],
        results[2][1],
        results[2][2],
        results[2][3],
        results[2][4],
        results[2][5],
        results[3][0],
        results[3][1],
        results[3][2],
        results[3][3],
        results[3][4],
        results[3][5],
    )


def solution(mesh):
    return jax.shard_map(
        on_device,
        mesh=mesh,
        in_specs=(
            P(None, ("group", "dp"), "tensor", None),
            P(None, ("group", "dp"), "tensor", None),
            P(None, ("group", "dp")),
            P(None, ("group", "dp"), None),
            P(None, ("group", "dp"), None, "tensor", None),
            P("group"),
            P("group", None, "dp", "tensor", None),
            P("group", None, "dp", "tensor", None),
            P("group", None, "dp", "tensor", None),
            P(None, "dp", "tensor", None),
            P(None, "dp", "tensor", None),
            P("group", None, "tensor", "dp", None),
            P("group", None, "tensor", "dp", None),
            P("group", None, "tensor", "dp", None),
            P(None, "tensor", "dp", None),
            P(None, "tensor", "dp", None),
            P("group", None, "tensor", "dp"),
            P("group", None, "tensor", "dp"),
            P("group", None, "tensor", "dp"),
            P(None, "tensor", "dp"),
            P(None, "tensor", "dp"),
            P("group", None, None, ("dp", "tensor")),
            P("group", None, None, ("dp", "tensor")),
            P("group", None, None, ("dp", "tensor")),
            P(None, None, ("dp", "tensor")),
            P(None, None, ("dp", "tensor")),
        ),
        out_specs=(
            P(None, ("group", "dp"), "tensor", None),
            P(None, ("group", "dp"), "tensor", None),
            P("group", None, "dp", "tensor", None),
            P("group", None, "dp", "tensor", None),
            P("group", None, "dp", "tensor", None),
            P(None, "dp", "tensor", None),
            P(None, "dp", "tensor", None),
            P(None, "dp", "tensor", None),
            P("group", None, "tensor", "dp", None),
            P("group", None, "tensor", "dp", None),
            P("group", None, "tensor", "dp", None),
            P(None, "tensor", "dp", None),
            P(None, "tensor", "dp", None),
            P(None, "tensor", "dp", None),
            P("group", None, "tensor", "dp"),
            P("group", None, "tensor", "dp"),
            P("group", None, "tensor", "dp"),
            P(None, "tensor", "dp"),
            P(None, "tensor", "dp"),
            P(None, "tensor", "dp"),
            P("group", None, None, ("dp", "tensor")),
            P("group", None, None, ("dp", "tensor")),
            P("group", None, None, ("dp", "tensor")),
            P(None, None, ("dp", "tensor")),
            P(None, None, ("dp", "tensor")),
            P(None, None, ("dp", "tensor")),
        ),
        check_vma=False,
    )
```

```python
import jax
import jax.numpy as jnp
from jax import lax
from jax.experimental import pallas as pl
from jax.experimental.pallas import tpu as pltpu
from jax.sharding import PartitionSpec as P

BETA_ONE = 0.9
BETA_TWO = 0.99
ADAM_EPS = 1e-08
LEARN_RATE = 0.04
DECAY_RATE = 0.1
OUTER_BETA = 0.9
OUTER_RATE = 0.7
NORM_EPS = 1e-06
MASKED = -1e30
MESH = pl.DeviceIdType.MESH
ZS = 4
F32, BF16 = jnp.float32, jnp.bfloat16


def place():
    d = lax.axis_index("dp")
    return d // 2, lax.rem(d, 2)


def neighbours():
    g, t = lax.axis_index("group"), lax.axis_index("tensor")
    z, x = place()
    return dict(
        x=(g, z * 2 + (1 - x), t),
        up=(g, (z + 1) * 2 + x, t),
        down=(g, (z - 1) * 2 + x, t),
        core=(g, z * 2 + x, 1 - t),
        group=(1 - g, z * 2 + x, t),
    )


def entry_barrier():
    z, _ = place()
    near = neighbours()
    bar = pltpu.get_barrier_semaphore()

    def greet(name):
        pl.semaphore_signal(bar, inc=1, device_id=near[name], device_id_type=MESH)

    for name in ("x", "core", "group"):
        greet(name)
    pl.when(z < ZS - 1)(lambda: greet("up"))
    pl.when(z > 0)(lambda: greet("down"))
    pl.semaphore_wait(bar, 3 + (z + 2) // 3 + (ZS + 1 - z) // 3)


WAYS = {"x": 0, "up": 1, "down": 2}


class Gather:
    def __init__(self, view, ssem, rsem):
        self.view, self.ssem, self.rsem = view, ssem, rsem
        self.near = neighbours()
        self.z, self.x = place()

    def copy(self, g, zsrc, xsrc, way):
        ref = self.view(g, zsrc * 2 + xsrc)
        return pltpu.make_async_remote_copy(
            src_ref=ref,
            dst_ref=ref,
            send_sem=self.ssem.at[g, zsrc, WAYS[way]],
            recv_sem=self.rsem.at[g, zsrc * 2 + xsrc],
            device_id=self.near[way],
            device_id_type=MESH,
        )

    def own(self, g, only=None):
        z, x = self.z, self.x
        ok = (z >= 0) if only is None else only(z)
        pl.when(ok)(lambda: self.copy(g, z, x, "x").start())
        pl.when(ok & (z < ZS - 1))(lambda: self.copy(g, z, x, "up").start())
        pl.when(ok & (z > 0))(lambda: self.copy(g, z, x, "down").start())

    def relay(self, g, k, only=None):
        z, x = self.z, self.x
        for way, src in (("up", z - k), ("down", z + k)):
            ok = (src >= 0) if way == "up" else (src < ZS)
            if only is not None:
                ok = ok & only(src)
            more = (z < ZS - 1) if way == "up" else (z > 0)

            @pl.when(ok)
            def _():
                self.copy(g, src, x, way).wait_recv()
                self.copy(g, src, x, "x").start()
                pl.when(more)(lambda: self.copy(g, src, x, way).start())

    def across(self, g, srcs=range(ZS)):
        for zsrc in srcs:
            self.copy(g, zsrc, 1 - self.x, "x").wait_recv()

    def drain(self, g, srcs=range(ZS)):
        z, x = self.z, self.x
        for zsrc in srcs:
            self.copy(g, zsrc, x, "x").wait_send()
            pl.when((zsrc <= z) & (z < ZS - 1))(lambda: self.copy(g, zsrc, x, "up").wait_send())
            pl.when((zsrc >= z) & (z > 0))(lambda: self.copy(g, zsrc, x, "down").wait_send())


def far_order(z, k):
    if k == 0:
        return 3 * (1 - z // 2)
    if k == 1:
        return lax.rem(2 + 3 * z, 5)
    if k == 2:
        return 1 + lax.rem(z, 2)
    return z


class Scatter:
    def __init__(self, source, xbuf, zbuf, xs, xr, zs, zr):
        self.source, self.xbuf, self.zbuf = source, xbuf, zbuf
        self.xs, self.xr, self.zs, self.zr = xs, xr, zs, zr
        self.near = neighbours()
        self.z, self.x = place()

    def xcopy(self, g, row):
        return pltpu.make_async_remote_copy(
            src_ref=self.source(g, row * 2 + (1 - self.x)),
            dst_ref=self.xbuf(g, row),
            send_sem=self.xs.at[g, row],
            recv_sem=self.xr.at[g, row],
            device_id=self.near["x"],
            device_id_type=MESH,
        )

    def zcopy(self, g, row, slot, way):
        return pltpu.make_async_remote_copy(
            src_ref=self.xbuf(g, row),
            dst_ref=self.zbuf(g, slot),
            send_sem=self.zs.at[g, row],
            recv_sem=self.zr.at[g, slot],
            device_id=self.near[way],
            device_id_type=MESH,
        )

    def send(self, g, k, only=None):
        row = far_order(self.z, k)
        ok = (row >= 0) if only is None else only(row)
        pl.when(ok)(lambda: self.xcopy(g, row).start())

    def pass_on(self, g, k, only=None):
        z, x = self.z, self.x
        row = far_order(z, k)
        ok = (row >= 0) if only is None else only(row)

        @pl.when(ok)
        def _():
            self.xcopy(g, row).wait_recv()
            below = z < row
            further = (below & (z > 0)) | ((z > row) & (z < ZS - 1))
            src, buf = self.source(g, row * 2 + x), self.xbuf(g, row)

            def add(*others):
                def body(i, _):
                    at = pl.ds(pl.multiple_of(i * 48, 48), 48)
                    total = buf[at, :].astype(F32)
                    for other in others:
                        total = total + other[at, :].astype(F32)
                    buf[at, :] = total.astype(BF16)
                    return 0

                lax.fori_loop(0, buf.shape[0] // 48, body, 0)

            @pl.when(further)
            def _():
                self.zcopy(g, row, row, "up").wait_recv()
                add(src, self.zbuf(g, row))

            @pl.when(jnp.logical_not(further))
            def _():
                add(src)

            pl.when(below & (z + 1 < row))(lambda: self.zcopy(g, row, row, "up").start())
            pl.when(below & (z + 1 == row))(lambda: self.zcopy(g, row, ZS, "up").start())
            pl.when(z > row)(lambda: self.zcopy(g, row, row, "down").start())

    def arrived(self, g):
        z = self.z
        self.xcopy(g, z).wait_recv()
        pl.when(z < ZS - 1)(lambda: self.zcopy(g, z, z, "down").wait_recv())
        pl.when(z > 0)(lambda: self.zcopy(g, z, ZS, "up").wait_recv())

    def drain(self, g, k, only=None):
        row = far_order(self.z, k)
        ok = (row >= 0) if only is None else only(row)

        @pl.when(ok)
        def _():
            self.xcopy(g, row).wait_send()
            if k < 3:
                self.zcopy(g, row, row, "up").wait_send()


VMEM_SPEC = pl.BlockSpec(memory_space=pltpu.VMEM)
SMEM_SPEC = pl.BlockSpec(memory_space=pltpu.SMEM)
ANY_SPEC = pl.BlockSpec(memory_space=pl.ANY)
DMA = pltpu.SemaphoreType.DMA
BIG_VMEM = 61 * 1024 * 1024
LANE = 128
GQKV, GUP, GNAR, GSMALL, GSUMS = range(5)


def mm(left, right, left_dim, right_dim):
    return lax.dot_general(
        left, right, (((left_dim,), (right_dim,)), ((), ())), preferred_element_type=F32
    )


def span(start, size, multiple):
    return pl.ds(pl.multiple_of(start, multiple), size)


def by_eights(values):
    rows, cols = values.shape
    return jnp.sum(values.reshape(rows // 8, 8, cols), axis=0)


def first_row(row):
    return row == 0


def other_rows(row):
    return row > 0


class Sizes:
    def __init__(self, x, wide_own, narrow_own, rand):
        self.micro, self.own, self.d = x.shape
        self.seq = 2 * self.own
        self.heads = rand.shape[1]
        self.dt = self.heads * 64
        self.ft = 2 * self.d
        self.wr = self.d // 8
        self.nr = narrow_own.shape[0]
        self.wc = 3 * self.dt + self.ft
        self.tiles = self.wc // LANE
        self.tokens = self.micro * self.seq


def layer_kernel(sz, *refs):
    (
        x_in, cot_in, lens, glob, rand, consts, small, w_lin, w_nar,
        f_lin, s_lin, a_lin, f_nar, s_nar, a_nar,
        out_ref, ingrad_ref, glin_out, gnar_out, mlin_out, mnar_out, small_out,
        wide, nar, xf, cot, qkv, mix, dmix, lse, mask, blocks,
        ps, pr, normed, scal, in2, uu, zb, drb, res, stage,
        gw, gn, xw, xn, zw, zn, glin, gnar, mlin, mnar, wn32,
        dsw, dsn, drw, drn, sm_all, sg_all, sm_mine, sm_peer, bias_row, norm_row, acc_b, acc_n,
        gsend, grecv, xs, xr, zs, zr, core_s, core_r, ys, yr, loc,
    ) = refs
    z, x = place()
    shard = z * 2 + x
    t = lax.axis_index("tensor")
    near = neighbours()
    D, DT, FT, OWN, SEQ, WR, NR = sz.d, sz.dt, sz.ft, sz.own, sz.seq, sz.wr, sz.nr
    QC = 3 * DT
    own_at = span(t * OWN, OWN, OWN)
    peer_at = span((1 - t) * OWN, OWN, OWN)

    def local(src, dst, sem):
        return pltpu.make_async_copy(src, dst, loc.at[sem])

    loads = [
        local(w_lin, uu.at[pl.ds(0, sz.tiles * WR)], 0),
        local(w_nar, wn32, 1),
        local(x_in.at[0], xf.at[0, own_at], 2),
        local(x_in.at[1], xf.at[1, own_at], 3),
        local(cot_in, cot, 4),
    ]
    for copy in loads:
        copy.start()
    entry_barrier()

    def halves(g):
        return pl.ds(0, QC) if g == GQKV else pl.ds(QC, FT)

    def view(g, s):
        if g == GNAR:
            return nar.at[span(s * NR, NR, NR)]
        if g == GSMALL:
            return sm_all.at[s]
        if g == GSUMS:
            return sg_all.at[s]
        return wide.at[span(s * WR, WR, WR), halves(g)]

    gat = Gather(view, gsend, grecv)

    def source(g, s):
        if g == GNAR:
            return gn.at[span(s * NR, NR, NR)]
        return gw.at[span(s * WR, WR, WR), halves(g)]

    sca = Scatter(
        source,
        lambda g, row: xn.at[row] if g == GNAR else xw.at[row, :, halves(g)],
        lambda g, row: zn.at[row] if g == GNAR else zw.at[row, :, halves(g)],
        xs, xr, zs, zr,
    )

    def core_copy(stage_at, src, dst):
        return pltpu.make_async_remote_copy(
            src_ref=src, dst_ref=dst, send_sem=core_s.at[stage_at], recv_sem=core_r.at[stage_at],
            device_id=near["core"], device_id_type=MESH,
        )

    def rows_copy(kind, m, ref):
        return core_copy(kind * 2 + m, ref.at[span(m * SEQ + t * OWN, OWN, OWN)],
                         ref.at[span(m * SEQ + t * OWN, OWN, OWN)])

    def part_copy(kind, m):
        return core_copy(kind * 2 + m, ps.at[m], pr.at[m])

    def x_copy(m):
        return core_copy(m, x_in.at[m], xf.at[m, own_at])

    for m in range(2):
        x_copy(m).start()

    sm_all[shard] = small[...]
    gat.own(GSMALL)
    loads[0].wait()

    def cast_tiles(lo, hi):
        def body(c, _):
            wide[span(shard * WR, WR, WR), span(c * LANE, LANE, LANE)] = uu[
                pl.ds(c, WR, stride=sz.tiles), :
            ].astype(BF16)
            return 0

        lax.fori_loop(lo, hi, body, 0)

    cast_tiles(0, QC // LANE)
    gat.own(GQKV)
    loads[1].wait()
    nar[span(shard * NR, NR, NR), :] = wn32[...].astype(BF16)
    gat.own(GNAR, first_row)
    cast_tiles(QC // LANE, sz.tiles)

    def build_masks():
        keys = lax.broadcasted_iota(jnp.int32, (SEQ, LANE), 0)
        lanes = lax.broadcasted_iota(jnp.int32, (SEQ, LANE), 1)
        kb = keys // 64
        blocks[...] = (kb == lanes).astype(F32).astype(BF16)
        for m in range(2):
            g0, g1 = glob[m, 0], glob[m, 1]
            base = (jnp.abs(kb - lanes) <= 1) | (kb == g0) | (kb == g1) | (lanes == g0) | (lanes == g1)
            real = keys < lens[m]

            def body(h, _):
                rows = rand[m, h]
                hit = base
                for r in range(3):
                    hit = hit | (kb == rows[r : r + 1, :])
                mask[m * sz.heads + h] = jnp.where(hit & real, 0.0, MASKED).astype(BF16)
                return 0

            lax.fori_loop(0, sz.heads, body, 0)

    gat.relay(GSMALL, 1)
    gat.relay(GQKV, 1)
    gat.own(GUP)
    build_masks()
    gat.relay(GSMALL, 2)
    gat.relay(GQKV, 2)
    gat.relay(GSMALL, 3)
    gat.relay(GQKV, 3)
    gat.relay(GNAR, 1, first_row)

    gat.across(GSMALL)
    total = sm_all[0].astype(F32)
    for s in range(1, 8):
        total = total + sm_all[s].astype(F32)
    sm_mine[...] = total

    def small_copy():
        return core_copy(2, sm_mine, sm_peer)

    small_copy().start()
    nb = bias_row.shape[1] // LANE
    small_copy().wait_recv()
    for c in range(nb):
        bias_row[0:1, c * LANE : (c + 1) * LANE] = sm_mine[c : c + 1, :]
    both = sm_mine[...] + sm_peer[...]
    for r in range(6):
        for c in range(D // LANE):
            at = nb + r * (D // LANE) + c
            norm_row[r : r + 1, c * LANE : (c + 1) * LANE] = both[at : at + 1, :]
    acc_b[...] = jnp.zeros_like(acc_b)
    acc_n[...] = jnp.zeros_like(acc_n)

    gat.across(GQKV)
    for m in range(2):
        loads[2 + m].wait()
        x_copy(m).wait_recv()
        for c in range(3):
            value = mm(xf[m], wide[:, c * DT : (c + 1) * DT], 1, 0)
            if c != 1:
                lo = 0 if c == 0 else DT
                value = value + bias_row[0:1, lo : lo + DT]
            qkv[m, :, c * DT : (c + 1) * DT] = value.astype(BF16)
        if m == 0:
            gat.relay(GNAR, 2, first_row)

    lane_low = lax.broadcasted_iota(jnp.int32, (1, LANE), 1) < 64

    def half(value, hh):
        return jnp.where(lane_low if hh == 0 else jnp.logical_not(lane_low), value, jnp.zeros_like(value))

    def pair_loads(m, p):
        return [qkv[m, :, span(c * DT + p * LANE, LANE, LANE)] for c in range(3)]

    def scores(m, p, hh, q, kh):
        head = m * sz.heads + p * 2 + hh
        kx = jnp.concatenate([kh, mask[head]], axis=1)
        qx = jnp.concatenate([q * jnp.asarray(0.125, BF16), blocks[...]], axis=1)
        return mm(kx, qx, 1, 1), head

    def attend(m):
        def body(p, _):
            q, k, v = pair_loads(m, p)
            out_t = jnp.zeros((LANE, SEQ), F32)
            for hh in range(2):
                s, head = scores(m, p, hh, q, half(k, hh))
                top = jnp.max(s, axis=0, keepdims=True)
                e = jnp.exp(s - top)
                total_e = jnp.sum(e, axis=0, keepdims=True)
                prob = (e * (1.0 / total_e)).astype(BF16)
                lse[head] = jnp.broadcast_to(top + jnp.log(total_e), (8, SEQ))
                out_t = out_t + mm(half(v, hh), prob, 0, 0)
            mix[span(m * SEQ, SEQ, SEQ), span(p * LANE, LANE, LANE)] = jnp.transpose(out_t).astype(BF16)
            return 0

        lax.fori_loop(0, sz.heads // 2, body, 0)

    gat.relay(GUP, 1)
    gat.own(GNAR, other_rows)
    attend(0)
    gat.relay(GNAR, 3, first_row)
    gat.relay(GUP, 2)
    attend(1)
    gat.relay(GUP, 3)

    def branch(m, left, right, right_dim, kind, add):
        value = mm(left[span(m * SEQ + (1 - t) * OWN, OWN, OWN), :], right, 1, right_dim)
        ps[m] = value
        part_copy(PARTS[kind], m).start()
        value = mm(left[span(m * SEQ + t * OWN, OWN, OWN), :], right, 1, right_dim)
        if add:
            res[m] += value
        else:
            res[m] = value

    gat.across(GNAR, [0])
    for m in range(2):
        branch(m, mix, nar[0:DT, :], 0, 0, False)

    def rows_loop(body):
        lax.fori_loop(0, OWN // 64, lambda i, c: (body(span(i * 64, 64, 64), i * 64), c)[1], 0)

    def stats(r):
        mean = jnp.mean(r, axis=1, keepdims=True)
        centred = r - mean
        var = jnp.mean(centred * centred, axis=1, keepdims=True)
        scaling = lax.rsqrt(var + NORM_EPS)
        return centred * scaling, scaling

    def norm(r):
        return norm_row[r : r + 1, :]

    def norm_one(m):
        part_copy(PARTS[0], m).wait()

        def body(rows, at):
            hidden = xf[m, span(t * OWN + at, 64, 64), :].astype(F32)
            n, scaling = stats(hidden + (res[m, rows, :] + pr[m, rows, :]) + norm(0))
            normed[m, rows, :] = n
            scal[m, rows, :] = scaling
            in2[span(m * SEQ + t * OWN + at, 64, 64), :] = (n * norm(2) + norm(3)).astype(BF16)

        rows_loop(body)
        rows_copy(ROWS[0], m, in2).start()

    for m in range(2):
        norm_one(m)
    gat.relay(GNAR, 1, other_rows)

    gat.across(GUP)

    def feed(m):
        rows_copy(ROWS[0], m, in2).wait()

        def body(c, _):
            value = mm(
                in2[span(m * SEQ, SEQ, SEQ), :], wide[:, span(QC + c * 256, 256, LANE)], 1, 0
            ) + bias_row[0:1, span(2 * DT + c * 256, 256, LANE)]
            square = value * value
            inner = GELU_A * value * (1.0 + GELU_B * square)
            tan = jnp.tanh(inner)
            hat = 0.5 * (1.0 + tan)
            zb[span(m * SEQ, SEQ, SEQ), span(c * 256, 256, 256)] = (value * hat).astype(BF16)
            slope = hat + 0.5 * value * (1.0 - tan * tan) * (GELU_A * (1.0 + 3.0 * GELU_B * square))
            for j in range(2):
                uu[span((c * 2 + j) * sz.tokens + m * SEQ, SEQ, SEQ), :] = slope[:, j * LANE : (j + 1) * LANE]
            return 0

        lax.fori_loop(0, FT // 256, body, 0)

    feed(0)
    gat.relay(GNAR, 2, other_rows)
    feed(1)
    gat.relay(GNAR, 3, other_rows)
    gat.across(GNAR, [1, 2, 3])
    for m in range(2):
        branch(m, zb, nar[DT:, :], 0, 1, False)

    loads[4].wait()

    def count(kind, value):
        acc_n[kind] += by_eights(value)

    def norm_back(grad, n, scaling, gain):
        scaled = grad * gain
        return scaling * (
            scaled
            - jnp.mean(scaled, axis=1, keepdims=True)
            - n * jnp.mean(scaled * n, axis=1, keepdims=True)
        )

    def norm_two(m):
        part_copy(PARTS[1], m).wait()

        def body(rows, at):
            first = normed[m, rows, :] * norm(2) + norm(3)
            n, scaling = stats(first + (res[m, rows, :] + pr[m, rows, :]) + norm(1))
            stage[m, rows, :] = n * norm(4) + norm(5)
            token = t * OWN + at + lax.broadcasted_iota(jnp.int32, (64, 1), 0)
            grad = jnp.where(token < lens[m], cot[m, rows, :].astype(F32), 0.0)
            count(4, grad * n)
            count(5, grad)
            back = norm_back(grad, n, scaling, norm(4))
            count(1, back)
            res[m, rows, :] = back
            drb[span(m * SEQ + t * OWN + at, 64, 64), :] = back.astype(BF16)

        rows_loop(body)
        rows_copy(ROWS[1], m, drb).start()

    def out_copy(m):
        return local(stage.at[m], out_ref.at[m], 5 + m)

    for m in range(2):
        norm_two(m)
        out_copy(m).start()

    for m in range(2):
        rows_copy(ROWS[1], m, drb).wait()

    def down_grad(c, _):
        gn[span(DT + c * 256, 256, LANE), :] = mm(zb[:, span(c * 256, 256, 256)], drb[...], 0, 0).astype(BF16)
        return 0

    lax.fori_loop(0, FT // 256, down_grad, 0)
    for k in range(4):
        sca.send(GNAR, k, other_rows)

    def feed_back(m):
        def body(c, _):
            grad = mm(
                drb[span(m * SEQ, SEQ, SEQ), :], nar[span(DT + c * 256, 256, LANE), :], 1, 1
            )
            slope = jnp.concatenate(
                [uu[span((c * 2 + j) * sz.tokens + m * SEQ, SEQ, SEQ), :] for j in range(2)], axis=1
            )
            low = (grad * slope).astype(BF16)
            zb[span(m * SEQ, SEQ, SEQ), span(c * 256, 256, 256)] = low
            acc_b[:, span(2 * DT + c * 256, 256, LANE)] += by_eights(low.astype(F32))
            return 0

        lax.fori_loop(0, FT // 256, body, 0)

    for m in range(2):
        feed_back(m)

    def up_grad(c, _):
        gw[span(c * 256, 256, 256), QC:] = mm(in2[:, span(c * 256, 256, 256)], zb[...], 0, 0).astype(BF16)
        return 0

    lax.fori_loop(0, D // 256, up_grad, 0)
    for k in range(4):
        sca.send(GUP, k)

    base = 3 * sz.tiles * WR
    tiles_n = D // LANE
    states = []
    for at, (lin, flat) in enumerate(((f_lin, f_nar), (s_lin, s_nar), (a_lin, a_nar))):
        states.append(local(lin, uu.at[pl.ds(at * sz.tiles * WR, sz.tiles * WR)], 7 + at))
        for c in range(tiles_n):
            states.append(
                local(
                    flat.at[:, pl.ds(c * LANE, LANE)],
                    uu.at[pl.ds(base + (at * tiles_n + c) * NR, NR)],
                    10 + at * tiles_n + c,
                )
            )
    states.append(local(w_lin, glin, 10 + 3 * tiles_n))
    for copy in states:
        copy.start()

    for m in range(2):
        branch(m, zb, wide[:, QC:], 1, 2, True)
    sca.pass_on(GNAR, 0, other_rows)

    def norm_one_back(m):
        part_copy(PARTS[2], m).wait()

        def body(rows, at):
            grad = res[m, rows, :] + pr[m, rows, :]
            n = normed[m, rows, :]
            count(2, grad * n)
            count(3, grad)
            back = norm_back(grad, n, scal[m, rows, :], norm(2))
            count(0, back)
            res[m, rows, :] = back
            drb[span(m * SEQ + t * OWN + at, 64, 64), :] = back.astype(BF16)

        rows_loop(body)
        rows_copy(ROWS[2], m, drb).start()

    for m in range(2):
        norm_one_back(m)
    for m in range(2):
        rows_copy(ROWS[2], m, drb).wait()
    gn[0:DT, :] = mm(mix[...], drb[...], 0, 0).astype(BF16)
    for k in range(4):
        sca.send(GNAR, k, first_row)
    for m in range(2):
        dmix[span(m * SEQ, SEQ, SEQ), :] = mm(
            drb[span(m * SEQ, SEQ, SEQ), :], nar[0:DT, :], 1, 1
        ).astype(BF16)
    sca.pass_on(GNAR, 1, other_rows)

    def attend_back(m):
        def body(p, _):
            q, k, v = pair_loads(m, p)
            do = dmix[span(m * SEQ, SEQ, SEQ), span(p * LANE, LANE, LANE)]
            dq_t = jnp.zeros((LANE, SEQ), F32)
            dk = jnp.zeros((SEQ, LANE), F32)
            dv = jnp.zeros((SEQ, LANE), F32)
            for hh in range(2):
                kh = half(k, hh)
                s, head = scores(m, p, hh, q, kh)
                prob = jnp.exp(s - lse[head][0:1, :])
                dp = mm(half(v, hh), do, 1, 1)
                centre = jnp.sum(prob * dp, axis=0, keepdims=True)
                ds = (prob * (dp - centre)).astype(BF16)
                dq_t = dq_t + mm(kh, ds, 0, 0)
                dk = dk + mm(ds, half(q, hh), 1, 0)
                dv = dv + mm(prob.astype(BF16), half(do, hh), 1, 0)
            for c, value in enumerate((jnp.transpose(dq_t) * 0.125, dk * 0.125, dv)):
                low = value.astype(BF16)
                qkv[m, :, span(c * DT + p * LANE, LANE, LANE)] = low
                if c != 1:
                    lo = 0 if c == 0 else DT
                    acc_b[:, span(lo + p * LANE, LANE, LANE)] += by_eights(low.astype(F32))
            return 0

        lax.fori_loop(0, sz.heads // 2, body, 0)

    attend_back(0)
    sca.pass_on(GNAR, 2, other_rows)
    attend_back(1)
    sca.pass_on(GUP, 0)

    def attn_grad(c, _):
        value = mm(xf[0, :, span(c * 256, 256, 256)], qkv[0], 0, 0)
        value = value + mm(xf[1, :, span(c * 256, 256, 256)], qkv[1], 0, 0)
        gw[span(c * 256, 256, 256), 0:QC] = value.astype(BF16)
        return 0

    lax.fori_loop(0, D // 256, attn_grad, 0)
    for k in range(4):
        sca.send(GQKV, k)

    sums = sg_all.at[shard]
    sums[...] = jnp.zeros((sg_all.shape[1], LANE), F32)
    flat = jnp.sum(acc_b[...], axis=0, keepdims=True)
    for c in range(nb):
        sums[c : c + 1, :] = flat[:, c * LANE : (c + 1) * LANE]
    for r in range(6):
        flat = jnp.sum(acc_n[r], axis=0, keepdims=True)
        for c in range(tiles_n):
            at = nb + r * tiles_n + c
            sums[at : at + 1, :] = flat[:, c * LANE : (c + 1) * LANE]
    gat.own(GSUMS)

    for m in range(2):
        out_copy(m).wait()

    def qkv_branch(m):
        right = wide[:, 0:QC]
        ps[m] = mm(qkv[m, peer_at, :], right, 1, 1)
        part_copy(PARTS[3], m).start()
        res[m] += mm(qkv[m, own_at, :], right, 1, 1)

    def ingrad_copy(m):
        return local(stage.at[m], ingrad_ref.at[m], 11 + 3 * tiles_n + m)

    for m in range(2):
        qkv_branch(m)
    sca.pass_on(GUP, 1)
    for k in range(1, 4):
        gat.relay(GSUMS, k)
    for m in range(2):
        part_copy(PARTS[3], m).wait()
        stage[m] = res[m] + pr[m]
        ingrad_copy(m).start()
    sca.pass_on(GUP, 2)
    for copy in states:
        copy.wait()

    one, two = consts[0], consts[1]

    def adam(weight, grad, first, second, anchor):
        first = BETA_ONE * first + (1.0 - BETA_ONE) * grad
        second = BETA_TWO * second + (1.0 - BETA_TWO) * grad * grad
        weight = weight - LEARN_RATE * (
            (first * one) / (jnp.sqrt(second * two) + ADAM_EPS) + DECAY_RATE * weight
        )
        return (anchor - weight).astype(BF16)

    def own_sum(srcs, at):
        value = srcs[0][:, at].astype(F32) + srcs[1][:, at].astype(F32)
        value = value + jnp.where(z < ZS - 1, srcs[2][:, at].astype(F32), 0.0)
        return value + jnp.where(z > 0, srcs[3][:, at].astype(F32), 0.0)

    def y_copy(g):
        src, dst = (dsn, drn) if g == GNAR else (dsw.at[:, halves(g)], drw.at[:, halves(g)])
        return pltpu.make_async_remote_copy(
            src_ref=src, dst_ref=dst, send_sem=ys.at[g], recv_sem=yr.at[g],
            device_id=near["group"], device_id_type=MESH,
        )

    def update_wide(g, lo, hi):
        sca.arrived(g)
        srcs = (gw.at[span(shard * WR, WR, WR)], xw.at[z], zw.at[z], zw.at[ZS])

        def body(c, _):
            at = span(c * LANE, LANE, LANE)
            lin = pl.ds(c, WR, stride=sz.tiles)
            grad = own_sum(srcs, at)
            weight = glin[lin, :]
            dsw[:, at] = adam(
                weight,
                grad,
                *(uu[pl.ds(n * sz.tiles * WR + c, WR, stride=sz.tiles), :] for n in range(3)),
            )
            glin[lin, :] = grad
            return 0

        lax.fori_loop(lo, hi, body, 0)
        y_copy(g).start()

    def update_narrow(only):
        @pl.when(only(z))
        def _():
            sca.arrived(GNAR)
            srcs = (gn.at[span(shard * NR, NR, NR)], xn.at[z], zn.at[z], zn.at[ZS])

            def body(c, _):
                at = span(c * LANE, LANE, LANE)
                grad = own_sum(srcs, at)
                gnar[:, at] = grad
                dsn[:, at] = adam(
                    wn32[:, at],
                    grad,
                    *(uu[span(base + (n * tiles_n + c) * NR, NR, 8), :] for n in range(3)),
                )
                return 0

            lax.fori_loop(0, tiles_n, body, 0)
            y_copy(GNAR).start()

    def mean_wide(g, lo, hi):
        y_copy(g).wait()

        def body(c, _):
            at = span(c * LANE, LANE, LANE)
            mlin[pl.ds(c, WR, stride=sz.tiles), :] = 0.5 * (
                dsw[:, at].astype(F32) + drw[:, at].astype(F32)
            )
            return 0

        lax.fori_loop(lo, hi, body, 0)

    split = QC // LANE
    update_narrow(other_rows)
    update_wide(GUP, split, sz.tiles)
    for k in range(3):
        sca.pass_on(GNAR, k, first_row)
    sca.pass_on(GQKV, 0)
    update_narrow(first_row)
    sca.pass_on(GQKV, 1)

    gat.across(GSUMS)
    total = sg_all[0]
    for s in range(1, 8):
        total = total + sg_all[s]
    small_copy().wait_send()
    sm_mine[...] = total

    def sums_copy():
        return core_copy(3, sm_mine, sm_peer)

    sums_copy().start()
    sca.pass_on(GQKV, 2)
    sums_copy().wait()
    row_at = lax.broadcasted_iota(jnp.int32, sm_mine.shape, 0)
    sm_mine[...] += jnp.where(row_at >= nb, sm_peer[...], 0.0)
    y_copy(GNAR).wait()
    mnar[...] = 0.5 * (dsn[...].astype(F32) + drn[...].astype(F32))
    mean_wide(GUP, split, sz.tiles)
    update_wide(GQKV, 0, split)
    last = 13 + 3 * tiles_n
    ends = [
        local(glin, glin_out, last),
        local(gnar, gnar_out, last + 1),
        local(mnar, mnar_out, last + 2),
        local(sm_mine, small_out, last + 3),
    ]
    for copy in ends:
        copy.start()
    mean_wide(GQKV, 0, split)
    tail = local(mlin, mlin_out, last + 4)
    tail.start()

    for g in range(5):
        gat.drain(g)
    for m in range(2):
        x_copy(m).wait_send()
        ingrad_copy(m).wait()
    for g in (GQKV, GUP, GNAR):
        for k in range(4):
            sca.drain(g, k)
    for copy in ends:
        copy.wait()
    tail.wait()


PARTS = (2, 3, 4, 5)
ROWS = (6, 7, 8)
GELU_A = 0.7978845608028654
GELU_B = 0.044715


def gelu_tanh(values):
    return jax.nn.gelu(values, approximate=True)


def norm_stats(values):
    average = jnp.mean(values, axis=-1, keepdims=True)
    centred = values - average
    spread = jnp.mean(centred * centred, axis=-1, keepdims=True)
    scaling = lax.rsqrt(spread + NORM_EPS)
    return (centred * scaling, scaling)


def norm_back(grad_rows, normed, scaling, gain):
    scaled = grad_rows * gain
    return scaling * (
        scaled
        - jnp.mean(scaled, axis=-1, keepdims=True)
        - normed * jnp.mean(scaled * normed, axis=-1, keepdims=True)
    )


def rows_forward(values):
    return lax.all_gather(values, "tensor", axis=0, tiled=True)


def sum_forward(values):
    return lax.psum_scatter(values, "tensor", scatter_dimension=0, tiled=True)


def rows_backward(values):
    return lax.all_gather(values, "tensor", axis=0, tiled=True)


def sum_backward(values):
    return lax.psum_scatter(values, "tensor", scatter_dimension=0, tiled=True)


def block_mask(global_pair, random_rows, block_total):
    block_ids = jnp.arange(block_total, dtype=jnp.int32)
    nearby = jnp.abs(block_ids[:, None] - block_ids[None, :]) <= 1
    global_hit = jnp.any(block_ids[:, None] == global_pair[None, :], axis=1)
    allowed_base = nearby | global_hit[None, :] | global_hit[:, None]
    chosen = jnp.any(
        jnp.transpose(random_rows, (1, 0, 2))[:, :, None, :] == block_ids[None, None, :, None],
        axis=3,
    )
    return allowed_base[None] | chosen


def split_blocks(blocks_ok, seq_len, block_len):
    heads_dev = blocks_ok.shape[0]
    query_rows = min(seq_len, 512)
    block_count = seq_len // query_rows
    per_rows = query_rows // block_len
    mask_parts = jnp.transpose(
        blocks_ok.reshape(heads_dev, block_count, per_rows, -1), (1, 0, 2, 3)
    )
    return (mask_parts, query_rows, block_count)


def attend_forward(queries, keys_all, values_all, blocks_ok, key_ok, block_len):
    seq_len, heads_dev, head_width = queries.shape
    scaling = head_width ** (-0.5)
    mask_parts, query_rows, block_count = split_blocks(blocks_ok, seq_len, block_len)
    query_parts = queries.reshape(block_count, query_rows, heads_dev, head_width)

    def per_block(operands):
        query_part, mask_part = operands
        allowed = (
            jnp.repeat(jnp.repeat(mask_part, block_len, axis=1), block_len, axis=2)
            & key_ok[None, None, :]
        )
        scores = (
            jnp.einsum("qhd,khd->hqk", query_part, keys_all, preferred_element_type=jnp.float32)
            * scaling
        )
        masked = jnp.where(allowed, scores, MASKED)
        highest = jnp.max(masked, axis=2, keepdims=True)
        weights_exp = jnp.exp(masked - highest)
        summed = jnp.sum(weights_exp, axis=2, keepdims=True)
        prob_rows = (weights_exp / summed).astype(jnp.bfloat16)
        outputs = jnp.einsum(
            "hqk,khd->qhd", prob_rows, values_all, preferred_element_type=jnp.float32
        )
        return (outputs, (highest + jnp.log(summed))[:, :, 0])

    outputs, log_totals = lax.map(per_block, (query_parts, mask_parts))
    return (outputs.reshape(seq_len, heads_dev * head_width), log_totals)


def attend_backward(
    queries, keys_all, values_all, grad_mixed, log_totals, blocks_ok, key_ok, block_len
):
    seq_len, heads_dev, head_width = queries.shape
    scaling = head_width ** (-0.5)
    mask_parts, query_rows, block_count = split_blocks(blocks_ok, seq_len, block_len)
    query_parts = queries.reshape(block_count, query_rows, heads_dev, head_width)
    grad_parts = grad_mixed.reshape(block_count, query_rows, heads_dev, head_width)

    def per_block(running, operands):
        key_total, value_total = running
        query_part, mask_part, grad_part, total_part = operands
        allowed = (
            jnp.repeat(jnp.repeat(mask_part, block_len, axis=1), block_len, axis=2)
            & key_ok[None, None, :]
        )
        scores = (
            jnp.einsum("qhd,khd->hqk", query_part, keys_all, preferred_element_type=jnp.float32)
            * scaling
        )
        prob_rows = jnp.exp(jnp.where(allowed, scores, MASKED) - total_part[:, :, None])
        grad_probs = jnp.einsum(
            "qhd,khd->hqk", grad_part, values_all, preferred_element_type=jnp.float32
        )
        centre = jnp.sum(prob_rows * grad_probs, axis=2, keepdims=True)
        grad_scores = (prob_rows * (grad_probs - centre)).astype(jnp.bfloat16)
        query_grad = (
            jnp.einsum("hqk,khd->qhd", grad_scores, keys_all, preferred_element_type=jnp.float32)
            * scaling
        )
        key_total = (
            key_total
            + jnp.einsum(
                "hqk,qhd->khd", grad_scores, query_part, preferred_element_type=jnp.float32
            )
            * scaling
        )
        value_total = value_total + jnp.einsum(
            "hqk,qhd->khd",
            prob_rows.astype(jnp.bfloat16),
            grad_part,
            preferred_element_type=jnp.float32,
        )
        return ((key_total, value_total), query_grad)

    zeros_init = jnp.zeros(keys_all.shape, jnp.float32)
    (key_grad, value_grad), query_grad = lax.scan(
        per_block, (zeros_init, zeros_init), (query_parts, mask_parts, grad_parts, log_totals)
    )
    flat = heads_dev * head_width
    return (
        query_grad.reshape(seq_len, flat),
        key_grad.reshape(seq_len, flat),
        value_grad.reshape(seq_len, flat),
    )


def adam_step(weight, gradient, first, second, count):
    first_new = BETA_ONE * first + (1.0 - BETA_ONE) * gradient
    second_new = BETA_TWO * second + (1.0 - BETA_TWO) * gradient * gradient
    first_hat = first_new / (1.0 - BETA_ONE**count)
    second_hat = second_new / (1.0 - BETA_TWO**count)
    weight_new = weight - LEARN_RATE * (
        first_hat / (jnp.sqrt(second_hat) + ADAM_EPS) + DECAY_RATE * weight
    )
    return (weight_new, first_new, second_new)


def general_path(
    layer_input,
    out_cotangent,
    lengths,
    global_blocks,
    rand_blocks,
    inner_steps,
    wide_inner,
    wide_first,
    wide_second,
    wide_anchor,
    wide_outer,
    narrow_inner,
    narrow_first,
    narrow_second,
    narrow_anchor,
    narrow_outer,
    bias_inner,
    bias_first,
    bias_second,
    bias_anchor,
    bias_outer,
    norms_inner,
    norms_first,
    norms_second,
    norms_anchor,
    norms_outer,
):
    micro_count = layer_input.shape[0]
    row_count = layer_input.shape[2]
    layers = wide_inner.shape[1]
    tensor_count = lax.axis_size("tensor")
    seq_len = row_count * tensor_count
    block_total = rand_blocks.shape[2]
    block_len = seq_len // block_total
    heads_dev = rand_blocks.shape[3]
    model_width = layer_input.shape[3]
    head_width = model_width // (heads_dev * tensor_count)
    attn_cols = heads_dev * head_width
    own_rows = lax.axis_index("tensor") * row_count + jnp.arange(row_count, dtype=jnp.int32)
    norms_full = lax.all_gather(
        norms_inner[0].astype(jnp.bfloat16), ("dp", "tensor"), axis=2, tiled=True
    ).astype(jnp.float32)
    outs_rows = []
    grads_rows = []
    collected = []
    collected_rows = []
    for micro_index in range(micro_count):
        weights = [
            (
                lax.all_gather(
                    wide_inner[0, 0, :, 0, :].astype(jnp.bfloat16), "dp", axis=0, tiled=True
                ),
                lax.all_gather(
                    narrow_inner[0, 0, 0].astype(jnp.bfloat16), "dp", axis=0, tiled=True
                ),
                lax.all_gather(bias_inner[0, 0, 0].astype(jnp.bfloat16), "dp", axis=0, tiled=True),
            )
        ]
        length = lengths[micro_index, 0]
        key_ok = jnp.arange(seq_len, dtype=jnp.int32) < length
        row_ok = (own_rows < length).astype(jnp.float32)[:, None]
        blocks_ok = block_mask(
            global_blocks[micro_index, 0], rand_blocks[micro_index, 0], block_total
        )
        hidden = layer_input[micro_index, 0].astype(jnp.float32)
        layer_index = 0
        w_wide, w_narrow, w_bias = weights[layer_index]
        bias_rows = w_bias.astype(jnp.float32)
        norm_rows = norms_full[layer_index]
        inputs_one = rows_forward(hidden.astype(jnp.bfloat16))
        qkv_bias = jnp.concatenate(
            [
                bias_rows[:attn_cols],
                jnp.zeros((attn_cols,), jnp.float32),
                bias_rows[attn_cols : 2 * attn_cols],
            ]
        )
        qkv = (
            jnp.dot(inputs_one, w_wide[:, : 3 * attn_cols], preferred_element_type=jnp.float32)
            + qkv_bias
        ).astype(jnp.bfloat16)
        queries = qkv[:, :attn_cols].reshape(seq_len, heads_dev, head_width)
        keys_all = qkv[:, attn_cols : 2 * attn_cols].reshape(seq_len, heads_dev, head_width)
        values_all = qkv[:, 2 * attn_cols :].reshape(seq_len, heads_dev, head_width)
        mixed, log_totals = attend_forward(
            queries, keys_all, values_all, blocks_ok, key_ok, block_len
        )
        mixed = mixed.astype(jnp.bfloat16)
        branch = sum_forward(
            jnp.dot(mixed, w_narrow[:attn_cols], preferred_element_type=jnp.float32)
        )
        normed, scaling = norm_stats(hidden + branch + norm_rows[0])
        first_out = normed * norm_rows[2] + norm_rows[3]
        inputs_two = rows_forward(first_out.astype(jnp.bfloat16))
        inner_pre = (
            jnp.dot(inputs_two, w_wide[:, 3 * attn_cols :], preferred_element_type=jnp.float32)
            + bias_rows[2 * attn_cols :]
        )
        gelu_vals, gelu_pull = jax.vjp(gelu_tanh, inner_pre)
        gelu_out = gelu_vals.astype(jnp.bfloat16)
        branch_two = sum_forward(
            jnp.dot(gelu_out, w_narrow[attn_cols:], preferred_element_type=jnp.float32)
        )
        normed_two, scaling_two = norm_stats(first_out + branch_two + norm_rows[1])
        stored = [
            (
                inputs_one,
                queries,
                keys_all,
                values_all,
                mixed,
                log_totals,
                normed,
                scaling,
                inputs_two,
                gelu_pull,
                gelu_out,
                normed_two,
                scaling_two,
            )
        ]
        hidden = normed_two * norm_rows[4] + norm_rows[5]
        outs_rows.append(hidden)
        grad_rows = out_cotangent[micro_index, 0].astype(jnp.float32) * row_ok
        pieces = [None] * layers
        for layer_index in reversed(range(layers)):
            (
                inputs_one,
                queries,
                keys_all,
                values_all,
                mixed,
                log_totals,
                normed,
                scaling,
                inputs_two,
                gelu_pull,
                gelu_out,
                normed_two,
                scaling_two,
            ) = stored[layer_index]
            w_wide, w_narrow, w_bias = weights[layer_index]
            norm_rows = norms_full[layer_index]
            gain_two_grad = jnp.sum(grad_rows * normed_two, axis=0)
            shift_two_grad = jnp.sum(grad_rows, axis=0)
            residual_two = norm_back(grad_rows, normed_two, scaling_two, norm_rows[4])
            down_bias_grad = jnp.sum(residual_two, axis=0)
            full_two = rows_backward(residual_two.astype(jnp.bfloat16))
            down_grad = jnp.einsum(
                "sf,sd->fd", gelu_out, full_two, preferred_element_type=jnp.float32
            )
            gelu_grad = jnp.einsum(
                "sd,fd->sf", full_two, w_narrow[attn_cols:], preferred_element_type=jnp.float32
            )
            inner_grad = gelu_pull(gelu_grad)[0].astype(jnp.bfloat16)
            up_bias_grad = jnp.sum(inner_grad, axis=0, dtype=jnp.float32)
            up_grad = jnp.einsum(
                "sd,sf->df", inputs_two, inner_grad, preferred_element_type=jnp.float32
            )
            first_grad = residual_two + sum_backward(
                jnp.einsum(
                    "sf,df->sd",
                    inner_grad,
                    w_wide[:, 3 * attn_cols :],
                    preferred_element_type=jnp.float32,
                )
            )
            gain_one_grad = jnp.sum(first_grad * normed, axis=0)
            shift_one_grad = jnp.sum(first_grad, axis=0)
            residual_one = norm_back(first_grad, normed, scaling, norm_rows[2])
            out_bias_grad = jnp.sum(residual_one, axis=0)
            full_one = rows_backward(residual_one.astype(jnp.bfloat16))
            out_grad = jnp.einsum("sa,sd->ad", mixed, full_one, preferred_element_type=jnp.float32)
            mixed_grad = jnp.einsum(
                "sd,ad->sa", full_one, w_narrow[:attn_cols], preferred_element_type=jnp.float32
            ).astype(jnp.bfloat16)
            query_grad, key_grad, value_grad = attend_backward(
                queries,
                keys_all,
                values_all,
                mixed_grad.reshape(seq_len, heads_dev, head_width),
                log_totals,
                blocks_ok,
                key_ok,
                block_len,
            )
            qkv_grad = jnp.concatenate([query_grad, key_grad, value_grad], axis=1).astype(
                jnp.bfloat16
            )
            query_bias_grad = jnp.sum(qkv_grad[:, :attn_cols], axis=0, dtype=jnp.float32)
            value_bias_grad = jnp.sum(qkv_grad[:, 2 * attn_cols :], axis=0, dtype=jnp.float32)
            attn_weight_grad = jnp.einsum(
                "sd,sc->dc", inputs_one, qkv_grad, preferred_element_type=jnp.float32
            )
            grad_rows = residual_one + sum_backward(
                jnp.einsum(
                    "sc,dc->sd",
                    qkv_grad,
                    w_wide[:, : 3 * attn_cols],
                    preferred_element_type=jnp.float32,
                )
            )
            pieces[layer_index] = (
                jnp.concatenate([attn_weight_grad, up_grad], axis=1),
                jnp.concatenate([out_grad, down_grad], axis=0),
                jnp.concatenate([query_bias_grad, value_bias_grad, up_bias_grad]),
                jnp.stack(
                    [
                        out_bias_grad,
                        down_bias_grad,
                        gain_one_grad,
                        shift_one_grad,
                        gain_two_grad,
                        shift_two_grad,
                    ]
                ),
            )
        grads_rows.append(grad_rows)
        micro_pieces = (
            jnp.stack([item[0] for item in pieces]),
            jnp.stack([item[1] for item in pieces]),
            jnp.stack([item[2] for item in pieces]),
        )
        collected_rows.append(jnp.stack([item[3] for item in pieces]))
        collected.append(micro_pieces)
    merged = collected[0]
    for extra in collected[1:]:
        merged = jax.tree.map(jnp.add, merged, extra)
    merged_rows = collected_rows[0]
    for extra in collected_rows[1:]:
        merged_rows = merged_rows + extra
    shards = (
        lax.psum_scatter(merged[0], "dp", scatter_dimension=1, tiled=True),
        lax.psum_scatter(merged[1], "dp", scatter_dimension=1, tiled=True),
        lax.psum_scatter(merged[2], "dp", scatter_dimension=1, tiled=True),
    )
    row_shard = lax.psum_scatter(merged_rows, ("dp", "tensor"), scatter_dimension=2, tiled=True)
    grads = (
        shards[0][None, :, :, None, :],
        shards[1][None, :, None],
        shards[2][None, :, None],
        row_shard[None],
    )
    inners = (wide_inner, narrow_inner, bias_inner, norms_inner)
    firsts = (wide_first, narrow_first, bias_first, norms_first)
    seconds = (wide_second, narrow_second, bias_second, norms_second)
    anchors = (wide_anchor, narrow_anchor, bias_anchor, norms_anchor)
    outers = (wide_outer, narrow_outer, bias_outer, norms_outer)
    count = inner_steps[0].astype(jnp.float32)
    updated = [
        adam_step(inners[kind], grads[kind], firsts[kind], seconds[kind], count)
        for kind in range(4)
    ]
    diffs = tuple((anchors[kind] - updated[kind][0][0] for kind in range(4)))
    diff_sums = lax.psum((diffs[0], diffs[1], diffs[2], diffs[3]), "group")
    group_count = lax.axis_size("group")
    results = []
    for kind in range(4):
        mean_diff = diff_sums[kind] / group_count
        outer_new = OUTER_BETA * outers[kind] + mean_diff
        anchor_new = anchors[kind] - OUTER_RATE * (mean_diff + OUTER_BETA * outer_new)
        results.append(
            (grads[kind], updated[kind][1], updated[kind][2], mean_diff, outer_new, anchor_new)
        )
    layer_out = jnp.stack(outs_rows)[:, None]
    input_grad = jnp.stack(grads_rows)[:, None]
    return (
        layer_out,
        input_grad,
        results[0][0],
        results[0][1],
        results[0][2],
        results[0][3],
        results[0][4],
        results[0][5],
        results[1][0],
        results[1][1],
        results[1][2],
        results[1][3],
        results[1][4],
        results[1][5],
        results[2][0],
        results[2][1],
        results[2][2],
        results[2][3],
        results[2][4],
        results[2][5],
        results[3][0],
        results[3][1],
        results[3][2],
        results[3][3],
        results[3][4],
        results[3][5],
    )


def finish_kernel(*refs):
    for at in (0, 6):
        grad, mean, first, second, anchor, outer = (ref[...] for ref in refs[at : at + 6])
        out = refs[12 + at : 18 + at]
        out[0][...] = grad
        out[1][...] = BETA_ONE * first + (1.0 - BETA_ONE) * grad
        out[2][...] = BETA_TWO * second + (1.0 - BETA_TWO) * grad * grad
        out[3][...] = mean
        outer_new = OUTER_BETA * outer + mean
        out[4][...] = outer_new
        out[5][...] = anchor - OUTER_RATE * (mean + OUTER_BETA * outer_new)


def finish(wide_set, narrow_set):
    steps = 6
    specs = []
    for arr in (wide_set[0], narrow_set[0]):
        rows, cols = arr.shape
        specs += [pl.BlockSpec((rows // steps, cols), lambda i: (i, 0))] * 6
    shapes = [jax.ShapeDtypeStruct(arr.shape, F32) for arr in (*wide_set, *narrow_set)]
    return pl.pallas_call(
        finish_kernel,
        grid=(steps,),
        in_specs=specs,
        out_specs=specs,
        out_shape=shapes,
        name="finish",
    )(*wide_set, *narrow_set)


def fast_path(mesh_sizes, args):
    (
        layer_input, out_cotangent, lengths, global_blocks, rand_blocks, inner_steps,
        wide_inner, wide_first, wide_second, wide_anchor, wide_outer,
        narrow_inner, narrow_first, narrow_second, narrow_anchor, narrow_outer,
        bias_inner, bias_first, bias_second, bias_anchor, bias_outer,
        norms_inner, norms_first, norms_second, norms_anchor, norms_outer,
    ) = args
    dp, tensor = lax.axis_index("dp"), lax.axis_index("tensor")
    x, cot = layer_input[:, 0], out_cotangent[:, 0]
    rand = jnp.transpose(rand_blocks[:, 0], (0, 2, 3, 1))
    rand = jnp.pad(rand, ((0, 0), (0, 0), (0, 5), (0, LANE - rand.shape[3])), constant_values=-1)

    def lin(values):
        return values.reshape(-1, LANE)

    def flat(values):
        return values.reshape(values.shape[-2:])

    wide_set = [lin(v) for v in (wide_inner, wide_first, wide_second, wide_anchor, wide_outer)]
    narrow_set = [flat(v) for v in (narrow_inner, narrow_first, narrow_second, narrow_anchor, narrow_outer)]
    bias_len, rows_len = bias_inner.shape[-1], norms_inner.shape[-1]
    bias_all, width = bias_len * 8, rows_len * 16
    count = inner_steps[0].astype(F32)
    consts = jnp.stack([1.0 / (1.0 - BETA_ONE**count), 1.0 / (1.0 - BETA_TWO**count)])
    bias_at, rows_at = dp * bias_len, (dp * 2 + tensor) * rows_len
    bias_low = lax.dynamic_update_slice(
        jnp.zeros((bias_all,), BF16), bias_inner[0, 0, 0].astype(BF16), (bias_at,)
    )
    rows_low = lax.dynamic_update_slice(
        jnp.zeros((6, width), BF16), norms_inner[0, 0].astype(BF16), (0, rows_at)
    )
    small = jnp.concatenate([bias_low.reshape(-1, LANE), rows_low.reshape(-1, LANE)])
    nb = bias_all // LANE
    used = small.shape[0]
    small = jnp.pad(small, ((0, -used % 16), (0, 0)))

    sz = Sizes(x, wide_set[0], narrow_set[0], rand)
    M, OWN, SEQ, D, DT, FT, WR, NR, WC = sz.micro, sz.own, sz.seq, sz.d, sz.dt, sz.ft, sz.wr, sz.nr, sz.wc
    vm = pltpu.VMEM
    deep = DT + FT
    scratch = [
        vm((D, WC), BF16),
        vm((deep, D), BF16),
        vm((M, SEQ, D), BF16),
        vm((M, OWN, D), BF16),
        vm((M, SEQ, 3 * DT), BF16),
        vm((M * SEQ, DT), BF16),
        vm((M * SEQ, DT), BF16),
        vm((M * sz.heads, 8, SEQ), F32),
        vm((M * sz.heads, SEQ, LANE), BF16),
        vm((SEQ, LANE), BF16),
        vm((M, OWN, D), F32),
        vm((M, OWN, D), F32),
        vm((M, OWN, D), F32),
        vm((M, OWN, 1), F32),
        vm((M * SEQ, D), BF16),
        vm((FT // LANE * M * SEQ, LANE), F32),
        vm((M * SEQ, FT), BF16),
        vm((M * SEQ, D), BF16),
        vm((M, OWN, D), F32),
        vm((M, OWN, D), F32),
        vm((D, WC), BF16),
        vm((deep, D), BF16),
        vm((ZS, WR, WC), BF16),
        vm((ZS, NR, D), BF16),
        vm((ZS + 1, WR, WC), BF16),
        vm((ZS + 1, NR, D), BF16),
        vm((sz.tiles * WR, LANE), F32),
        vm((NR, D), F32),
        vm((sz.tiles * WR, LANE), F32),
        vm((NR, D), F32),
        vm((NR, D), F32),
        vm((WR, WC), BF16),
        vm((NR, D), BF16),
        vm((WR, WC), BF16),
        vm((NR, D), BF16),
        vm((8, *small.shape), BF16),
        vm((8, *small.shape), F32),
        vm(small.shape, F32),
        vm(small.shape, F32),
        vm((8, bias_all), F32),
        vm((8, D), F32),
        vm((8, bias_all), F32),
        vm((6, 8, D), F32),
        DMA((5, ZS, 3)),
        DMA((5, 8)),
        DMA((3, ZS)),
        DMA((3, ZS)),
        DMA((3, ZS)),
        DMA((3, ZS + 1)),
        DMA((18,)),
        DMA((18,)),
        DMA((3,)),
        DMA((3,)),
        DMA((18 + 3 * (D // LANE),)),
    ]
    shape = jax.ShapeDtypeStruct
    lin_shape, flat_shape = shape((sz.tiles * WR, LANE), F32), shape((NR, D), F32)
    layer_out, input_grad, glin, gnar, mlin, mnar, sums = pl.pallas_call(
        lambda *refs: layer_kernel(sz, *refs),
        out_shape=(
            shape((M, OWN, D), F32), shape((M, OWN, D), F32),
            lin_shape, flat_shape, lin_shape, flat_shape, shape(small.shape, F32),
        ),
        in_specs=[
            ANY_SPEC, ANY_SPEC, SMEM_SPEC, SMEM_SPEC, VMEM_SPEC, SMEM_SPEC, VMEM_SPEC,
            *([ANY_SPEC] * 8),
        ],
        out_specs=(ANY_SPEC,) * 7,
        scratch_shapes=scratch,
        compiler_params=pltpu.CompilerParams(
            collective_id=1, has_side_effects=True, vmem_limit_bytes=BIG_VMEM
        ),
        name="layer_step",
    )(
        x, cot, lengths[:, 0], global_blocks[:, 0], rand, consts, small,
        wide_set[0], narrow_set[0], *wide_set[1:4], *narrow_set[1:4],
    )

    done = finish((glin, mlin, *wide_set[1:5]), (gnar, mnar, *narrow_set[1:5]))

    bias_grad = lax.dynamic_slice(sums[:nb].reshape(-1), (bias_at,), (bias_len,))
    rows_grad = lax.dynamic_slice(sums[nb:used].reshape(6, width), (0, rows_at), (6, rows_len))
    results = []
    for grad, inner, first, second, anchor, outer in (
        (bias_grad, bias_inner, bias_first, bias_second, bias_anchor, bias_outer),
        (rows_grad, norms_inner, norms_first, norms_second, norms_anchor, norms_outer),
    ):
        grad = grad.reshape(inner.shape)
        weight, first_new, second_new = adam_step(inner, grad, first, second, count)
        results.append([grad, first_new, second_new, anchor - weight[0], anchor, outer])
    sent = [item[3] for item in results]
    sums_of = lax.psum(tuple(sent), "group")
    smalls = []
    for item, total in zip(results, sums_of):
        mean_diff = total / 2
        outer_new = OUTER_BETA * item[5] + mean_diff
        anchor_new = item[4] - OUTER_RATE * (mean_diff + OUTER_BETA * outer_new)
        smalls += [item[0], item[1], item[2], mean_diff, outer_new, anchor_new]
    like = lambda values, kinds: [v.reshape(k.shape) for v, k in zip(values, kinds)]
    wide_out = like(done[:6], [wide_inner] * 3 + [wide_anchor] * 3)
    narrow_out = like(done[6:], [narrow_inner] * 3 + [narrow_anchor] * 3)
    return (layer_out[:, None], input_grad[:, None], *wide_out, *narrow_out, *smalls)


def on_device(*args):
    layer_input, rand_blocks, wide_inner, narrow_inner = args[0], args[4], args[6], args[11]
    heads, tokens, width = rand_blocks.shape[3], layer_input.shape[2], layer_input.shape[3]
    fits = (
        (lax.axis_size("dp"), lax.axis_size("tensor"), lax.axis_size("group")) == (8, 2, 2)
        and layer_input.shape[:2] == (2, 1)
        and wide_inner.shape[1] == 1
        and rand_blocks.shape[2] == 8
        and tokens == 256
        and width == heads * 2 * 64
        and heads % 2 == 0
        and wide_inner.shape[4] == 3 * heads * 64 + 2 * width
        and wide_inner.shape[2] % 48 == 0
        and narrow_inner.shape[3] % 48 == 0
        and width % 256 == 0
    )
    return fast_path(None, args) if fits else general_path(*args)


def solution(mesh):
    return jax.shard_map(
        on_device,
        mesh=mesh,
        in_specs=(
            P(None, ("group", "dp"), "tensor", None),
            P(None, ("group", "dp"), "tensor", None),
            P(None, ("group", "dp")),
            P(None, ("group", "dp"), None),
            P(None, ("group", "dp"), None, "tensor", None),
            P("group"),
            P("group", None, "dp", "tensor", None),
            P("group", None, "dp", "tensor", None),
            P("group", None, "dp", "tensor", None),
            P(None, "dp", "tensor", None),
            P(None, "dp", "tensor", None),
            P("group", None, "tensor", "dp", None),
            P("group", None, "tensor", "dp", None),
            P("group", None, "tensor", "dp", None),
            P(None, "tensor", "dp", None),
            P(None, "tensor", "dp", None),
            P("group", None, "tensor", "dp"),
            P("group", None, "tensor", "dp"),
            P("group", None, "tensor", "dp"),
            P(None, "tensor", "dp"),
            P(None, "tensor", "dp"),
            P("group", None, None, ("dp", "tensor")),
            P("group", None, None, ("dp", "tensor")),
            P("group", None, None, ("dp", "tensor")),
            P(None, None, ("dp", "tensor")),
            P(None, None, ("dp", "tensor")),
        ),
        out_specs=(
            P(None, ("group", "dp"), "tensor", None),
            P(None, ("group", "dp"), "tensor", None),
            P("group", None, "dp", "tensor", None),
            P("group", None, "dp", "tensor", None),
            P("group", None, "dp", "tensor", None),
            P(None, "dp", "tensor", None),
            P(None, "dp", "tensor", None),
            P(None, "dp", "tensor", None),
            P("group", None, "tensor", "dp", None),
            P("group", None, "tensor", "dp", None),
            P("group", None, "tensor", "dp", None),
            P(None, "tensor", "dp", None),
            P(None, "tensor", "dp", None),
            P(None, "tensor", "dp", None),
            P("group", None, "tensor", "dp"),
            P("group", None, "tensor", "dp"),
            P("group", None, "tensor", "dp"),
            P(None, "tensor", "dp"),
            P(None, "tensor", "dp"),
            P(None, "tensor", "dp"),
            P("group", None, None, ("dp", "tensor")),
            P("group", None, None, ("dp", "tensor")),
            P("group", None, None, ("dp", "tensor")),
            P(None, None, ("dp", "tensor")),
            P(None, None, ("dp", "tensor")),
            P(None, None, ("dp", "tensor")),
        ),
        check_vma=False,
    )
```

```python
import math

import jax
import jax.numpy as jnp
from jax import lax
from jax.experimental import pallas as pl
from jax.experimental.pallas import tpu as pltpu
from jax.sharding import PartitionSpec as P

BETA_ONE = 0.9
BETA_TWO = 0.99
ADAM_EPS = 1e-08
LEARN_RATE = 0.04
DECAY_RATE = 0.1
OUTER_BETA = 0.9
OUTER_RATE = 0.7
NORM_EPS = 1e-06
MASKED = -1e30
MESH = pl.DeviceIdType.MESH
ZS = 4
F32, BF16 = jnp.float32, jnp.bfloat16


def place():
    d = lax.axis_index("dp")
    return d // 2, lax.rem(d, 2)


def neighbours():
    g, t = lax.axis_index("group"), lax.axis_index("tensor")
    z, x = place()
    return dict(
        x=(g, z * 2 + (1 - x), t),
        up=(g, (z + 1) * 2 + x, t),
        down=(g, (z - 1) * 2 + x, t),
        pair=(g, (z + 1 - 2 * lax.rem(z, 2)) * 2 + x, t),
        core=(g, z * 2 + x, 1 - t),
        group=(1 - g, z * 2 + x, t),
    )


def greet():
    z, _ = place()
    near = neighbours()
    bar = pltpu.get_barrier_semaphore()

    def signal(name):
        pl.semaphore_signal(bar, inc=1, device_id=near[name], device_id_type=MESH)

    for name in ("x", "core", "group"):
        signal(name)
    pl.when(z < ZS - 1)(lambda: signal("up"))
    pl.when(z > 0)(lambda: signal("down"))


def barrier_wait():
    z, _ = place()
    pl.semaphore_wait(pltpu.get_barrier_semaphore(), 3 + (z + 2) // 3 + (ZS + 1 - z) // 3)


WAYS = {"x": 0, "up": 1, "down": 2, "pair": 3}


def direct(z, row, crossing):
    return not crossing or not ((row == 3 and z % 2 == 0) or (row == 0 and z % 2 == 1))


def crosses(z, row):
    return z % 2 == (0 if row == 0 else 1)


def onward(z, row):
    if row < z < ZS - 1:
        return "up"
    return "down" if 0 < z < row else None


def far_order(z, k):
    if k == 0:
        return 3 * (1 - z // 2)
    if k == 1:
        return 2 - z // 2
    if k == 2:
        return z + 1 - 2 * lax.rem(z, 2)
    return z


class Gather:
    def __init__(self, view, ssem, rsem, crossing):
        self.view, self.ssem, self.rsem, self.crossing = view, ssem, rsem, crossing
        self.near = neighbours()
        self.x = place()[1]

    def copy(self, g, row, column, way):
        ref = self.view(g, row * 2 + column)
        return pltpu.make_async_remote_copy(
            src_ref=ref,
            dst_ref=ref,
            send_sem=self.ssem.at[g, row, WAYS[way]],
            recv_sem=self.rsem.at[g, row * 2 + column],
            device_id=self.near[way],
            device_id_type=MESH,
        )

    def own(self, z, g):
        if direct(z, z, g in self.crossing):
            self.copy(g, z, self.x, "x").start()
        if z < ZS - 1:
            self.copy(g, z, self.x, "up").start()
        if z > 0:
            self.copy(g, z, self.x, "down").start()

    def relay(self, z, g, row):
        self.copy(g, row, self.x, "x").wait_recv()
        if direct(z, row, g in self.crossing):
            self.copy(g, row, self.x, "x").start()
        if onward(z, row):
            self.copy(g, row, self.x, onward(z, row)).start()

    def cross(self, g, row):
        self.copy(g, row, 1 - self.x, "x").wait_recv()
        self.copy(g, row, 1 - self.x, "pair").start()

    def across(self, z, g, rows=range(ZS)):
        for row in rows:
            if not (g in self.crossing and row in (0, 3) and crosses(z, row)):
                self.copy(g, row, 1 - self.x, "x").wait_recv()

    def drain(self, z, g):
        for row in range(ZS):
            if direct(z, row, g in self.crossing):
                self.copy(g, row, self.x, "x").wait_send()
            if row == z:
                if z < ZS - 1:
                    self.copy(g, row, self.x, "up").wait_send()
                if z > 0:
                    self.copy(g, row, self.x, "down").wait_send()
            elif onward(z, row):
                self.copy(g, row, self.x, onward(z, row)).wait_send()
            if g in self.crossing and row in (0, 3) and crosses(z, row):
                self.copy(g, row, 1 - self.x, "pair").wait_send()


class Scatter:
    def __init__(self, source, xbuf, zbuf, xs, xr, zs, zr, crossing, rows):
        self.source, self.xbuf, self.zbuf = source, xbuf, zbuf
        self.xs, self.xr, self.zs, self.zr = xs, xr, zs, zr
        self.crossing, self.rows = crossing, rows
        self.near = neighbours()
        self.z, self.x = place()

    def xcopy(self, g, row):
        return pltpu.make_async_remote_copy(
            src_ref=self.source(g, row * 2 + (1 - self.x)),
            dst_ref=self.xbuf(g, row),
            send_sem=self.xs.at[g, row],
            recv_sem=self.xr.at[g, row],
            device_id=self.near["x"],
            device_id_type=MESH,
        )

    def zcopy(self, g, row, slot, way):
        return pltpu.make_async_remote_copy(
            src_ref=self.xbuf(g, row),
            dst_ref=self.zbuf(g, slot),
            send_sem=self.zs.at[g, row],
            recv_sem=self.zr.at[g, slot],
            device_id=self.near[way],
            device_id_type=MESH,
        )

    def pair_copy(self, g, row):
        return pltpu.make_async_remote_copy(
            src_ref=self.source(g, row * 2 + (1 - self.x)),
            dst_ref=self.zbuf(g, ZS + 1),
            send_sem=self.zs.at[g, ZS],
            recv_sem=self.zr.at[g, ZS + 1],
            device_id=self.near["pair"],
            device_id_type=MESH,
        )

    def add(self, out, first, *others):
        size = 48 if out.shape[0] % 48 == 0 else 16

        def body(i, _):
            at = pl.ds(pl.multiple_of(i * size, size), size)
            total = first[at, :].astype(F32)
            for other in others:
                total = total + other[at, :].astype(F32)
            out[at, :] = total.astype(BF16)
            return 0

        lax.fori_loop(0, out.shape[0] // size, body, 0)

    def send(self, g):
        if g in self.crossing:
            odd = lax.rem(self.z, 2)
            pl.when(odd == 0)(lambda: self.pair_copy(g, 3).start())
            pl.when(odd == 1)(lambda: self.pair_copy(g, 0).start())
        for k in range(ZS):
            row = far_order(self.z, k)
            if g in self.crossing:
                pl.when((row > 0) & (row < ZS - 1))(lambda: self.xcopy(g, row).start())
            elif len(self.rows[g]) == ZS:
                self.xcopy(g, row).start()
            elif self.rows[g] == (0,):
                pl.when(row == 0)(lambda: self.xcopy(g, row).start())
            else:
                pl.when(row > 0)(lambda: self.xcopy(g, row).start())

    def merge(self, g, row):
        self.pair_copy(g, row).wait_recv()
        src = self.source(g, row * 2 + (1 - self.x))
        self.add(src, src, self.zbuf(g, ZS + 1))
        self.xcopy(g, row).start()

    def pass_on(self, z, g, row):
        parts, buf = [self.source(g, row * 2 + self.x)], self.xbuf(g, row)
        if direct(z, row, g in self.crossing):
            self.xcopy(g, row).wait_recv()
            parts.append(buf)
        if 0 < z < row or row < z < ZS - 1:
            self.zcopy(g, row, row, "up").wait_recv()
            parts.append(self.zbuf(g, row))
        self.add(buf, *parts)
        if z > row:
            self.zcopy(g, row, row, "down").start()
        else:
            self.zcopy(g, row, ZS if z + 1 == row else row, "up").start()

    def arrived(self, z, g):
        self.xcopy(g, z).wait_recv()
        parts = [self.source(g, z * 2 + self.x), self.xbuf(g, z)]
        if z < ZS - 1:
            self.zcopy(g, z, z, "down").wait_recv()
            parts.append(self.zbuf(g, z))
        if z > 0:
            self.zcopy(g, z, ZS, "up").wait_recv()
            parts.append(self.zbuf(g, ZS))
        return parts

    def drain(self, z, g):
        for row in self.rows[g]:
            if direct(z, row, g in self.crossing):
                self.xcopy(g, row).wait_send()
            if z != row:
                self.zcopy(g, row, row, "up").wait_send()
            if g in self.crossing and row in (0, 3) and not crosses(z, row):
                self.pair_copy(g, row).wait_send()


VMEM_SPEC = pl.BlockSpec(memory_space=pltpu.VMEM)
SMEM_SPEC = pl.BlockSpec(memory_space=pltpu.SMEM)
ANY_SPEC = pl.BlockSpec(memory_space=pl.ANY)
DMA = pltpu.SemaphoreType.DMA
BIG_VMEM = 61 * 1024 * 1024
LANE = 128
GQKV, GUP, GNAR, GSMALL = range(4)
SQKV, SUP, SNAR, SFIRST = (0, 1, 2), (3, 4), 5, (6, 7, 8)
ROWS_OF = {g: (0, 1, 2, 3) for g in (*SQKV, *SUP)} | {SNAR: (1, 2, 3)} | {g: (0,) for g in SFIRST}
BEGIN, RELAY, CROSS, PASS, MERGE, FINAL, PAIRED, ALONG = range(8)
AT_CAST = 0
AT_MASKS = 1
AT_SMALLS = 2
AT_QKV = 3
AT_ATTEND = 5
AT_BRANCH = 11
AT_NORM = 12
AT_FEED = 13
AT_DOWN = 17
AT_DOWN_GRAD = 18
AT_FEED_BACK = 19
AT_UP_GRAD = 21
AT_UP_BACK = 22
AT_NORM_BACK = 23
AT_OUT_GRAD = 24
AT_OUT_BACK = 25
AT_ATTEND_BACK = 26
AT_SUMS = 32
AT_QKV_GRAD = 33
AT_QKV_BACK = 34
AT_INPUT_GRAD = 35
AT_END = 36
PLAN = {
    AT_CAST: (
        (
            (BEGIN, GSMALL, 0),
            (BEGIN, GQKV, 0),
        ),
        (
            (BEGIN, GSMALL, 1),
            (BEGIN, GQKV, 1),
        ),
        (
            (BEGIN, GSMALL, 2),
            (BEGIN, GQKV, 2),
        ),
        (
            (BEGIN, GSMALL, 3),
            (BEGIN, GQKV, 3),
        ),
    ),
    AT_SMALLS: (
        (
            (RELAY, GSMALL, 1),
            (BEGIN, GNAR, 0),
            (CROSS, GQKV, 0),
            (RELAY, GQKV, 1),
            (RELAY, GSMALL, 2),
            (RELAY, GUP, 1),
            (RELAY, GQKV, 2),
            (RELAY, GSMALL, 3),
            (RELAY, GUP, 2),
            (RELAY, GQKV, 3),
        ),
        (
            (RELAY, GSMALL, 0),
            (RELAY, GSMALL, 2),
            (BEGIN, GUP, 1),
            (RELAY, GQKV, 0),
            (RELAY, GQKV, 2),
            (RELAY, GSMALL, 3),
            (RELAY, GUP, 2),
            (RELAY, GNAR, 0),
            (RELAY, GQKV, 3),
        ),
        (
            (RELAY, GSMALL, 1),
            (RELAY, GSMALL, 3),
            (BEGIN, GUP, 2),
            (RELAY, GQKV, 1),
            (RELAY, GQKV, 3),
            (RELAY, GSMALL, 0),
            (RELAY, GUP, 3),
            (RELAY, GUP, 1),
            (RELAY, GQKV, 0),
        ),
        (
            (RELAY, GSMALL, 2),
            (BEGIN, GUP, 3),
            (CROSS, GQKV, 3),
            (RELAY, GQKV, 2),
            (RELAY, GSMALL, 1),
            (RELAY, GUP, 2),
            (RELAY, GQKV, 1),
            (RELAY, GSMALL, 0),
            (RELAY, GUP, 1),
            (RELAY, GQKV, 0),
        ),
    ),
    AT_QKV: (
        (
            (BEGIN, GUP, 0),
            (RELAY, GUP, 3),
        ),
        (
            (RELAY, GUP, 3),
            (CROSS, GQKV, 3),
        ),
        (
            (RELAY, GNAR, 0),
            (CROSS, GQKV, 0),
        ),
        (
            (BEGIN, GNAR, 3),
            (RELAY, GNAR, 0),
        ),
    ),
    AT_QKV + 1: (
        (),
        (
            (BEGIN, GNAR, 1),
        ),
        (),
        (),
    ),
    AT_ATTEND: (
        (),
        (
            (RELAY, GUP, 0),
        ),
        (
            (BEGIN, GNAR, 2),
        ),
        (),
    ),
    AT_ATTEND + 1: (
        (),
        (),
        (
            (RELAY, GNAR, 3),
        ),
        (),
    ),
    AT_ATTEND + 4: (
        (
            (RELAY, GNAR, 1),
        ),
        (),
        (),
        (
            (RELAY, GNAR, 2),
        ),
    ),
    AT_NORM: (
        (),
        (
            (RELAY, GNAR, 2),
        ),
        (
            (RELAY, GNAR, 1),
        ),
        (),
    ),
    AT_FEED: (
        (
            (RELAY, GNAR, 2),
        ),
        (
            (RELAY, GNAR, 3),
        ),
        (
            (RELAY, GUP, 0),
        ),
        (
            (RELAY, GNAR, 1),
            (RELAY, GUP, 0),
        ),
    ),
    AT_DOWN: (
        (
            (RELAY, GNAR, 3),
        ),
        (),
        (),
        (),
    ),
    AT_UP_BACK: (
        (
            (PASS, SUP[0], 3),
        ),
        (),
        (),
        (
            (PASS, SUP[0], 0),
        ),
    ),
    AT_NORM_BACK: (
        (
            (PASS, SNAR, 3),
            (MERGE, SUP[0], 0),
        ),
        (),
        (),
        (
            (PASS, SNAR, 1),
        ),
    ),
    AT_OUT_GRAD: (
        (),
        (),
        (
            (MERGE, SUP[0], 0),
        ),
        (
            (MERGE, SUP[0], 3),
        ),
    ),
    AT_OUT_BACK: (
        (
            (PASS, SNAR, 2),
            (MERGE, SUP[1], 0),
            (PASS, SUP[1], 3),
        ),
        (
            (MERGE, SUP[0], 3),
        ),
        (),
        (
            (PASS, SNAR, 2),
            (PASS, SUP[1], 0),
        ),
    ),
    AT_ATTEND_BACK + 1: (
        (),
        (),
        (),
        (
            (MERGE, SUP[1], 3),
        ),
    ),
    AT_ATTEND_BACK + 3: (
        (
            (PASS, SNAR, 1),
        ),
        (),
        (),
        (),
    ),
    AT_ATTEND_BACK + 4: (
        (
            (PASS, SUP[0], 2),
        ),
        (),
        (
            (PASS, SNAR, 1),
        ),
        (),
    ),
    AT_ATTEND_BACK + 5: (
        (),
        (
            (PASS, SNAR, 3),
        ),
        (
            (MERGE, SUP[1], 0),
        ),
        (
            (PASS, SUP[0], 1),
        ),
    ),
    AT_SUMS: (
        (
            (PASS, SUP[0], 1),
        ),
        (),
        (),
        (
            (PASS, SUP[0], 2),
        ),
    ),
    AT_QKV_GRAD: (
        (),
        (
            (MERGE, SUP[1], 3),
        ),
        (
            (PASS, SNAR, 3),
        ),
        (),
    ),
    AT_INPUT_GRAD: (
        (),
        (),
        (
            (PASS, SUP[0], 0),
        ),
        (
            (PASS, SFIRST[0], 0),
        ),
    ),
    AT_END: (
        (
            (PASS, SUP[1], 2),
            (PASS, SUP[1], 1),
            (FINAL, SUP[0], 0),
            (PAIRED, GSMALL, 0),
            (ALONG, GSMALL, 1),
            (PASS, SQKV[0], 3),
            (PASS, SQKV[0], 2),
            (PASS, SQKV[0], 1),
            (FINAL, SFIRST[0], 0),
            (PASS, SQKV[1], 3),
            (FINAL, SFIRST[1], 0),
            (PASS, SQKV[1], 2),
            (PASS, SQKV[1], 1),
            (FINAL, SFIRST[2], 0),
            (PASS, SQKV[2], 3),
            (FINAL, SUP[1], 0),
            (PASS, SQKV[2], 2),
            (ALONG, GSMALL, 2),
            (ALONG, GSMALL, 3),
            (PASS, SQKV[2], 1),
            (FINAL, SQKV[0], 0),
            (FINAL, SQKV[1], 0),
            (FINAL, SQKV[2], 0),
        ),
        (
            (PASS, SNAR, 2),
            (PASS, SUP[0], 0),
            (FINAL, SNAR, 1),
            (PAIRED, GSMALL, 1),
            (PASS, SUP[0], 3),
            (PASS, SUP[0], 2),
            (PASS, SUP[1], 3),
            (FINAL, SUP[0], 1),
            (PASS, SFIRST[0], 0),
            (PASS, SUP[1], 2),
            (PASS, SFIRST[1], 0),
            (ALONG, GSMALL, 0),
            (PASS, SFIRST[2], 0),
            (PASS, SQKV[0], 3),
            (PASS, SQKV[0], 2),
            (PASS, SUP[1], 0),
            (ALONG, GSMALL, 2),
            (PASS, SQKV[1], 3),
            (PASS, SQKV[1], 2),
            (FINAL, SUP[1], 1),
            (ALONG, GSMALL, 3),
            (PASS, SQKV[0], 0),
            (PASS, SQKV[2], 3),
            (FINAL, SQKV[0], 1),
            (PASS, SQKV[2], 2),
            (PASS, SQKV[1], 0),
            (FINAL, SQKV[1], 1),
            (PASS, SQKV[2], 0),
            (FINAL, SQKV[2], 1),
        ),
        (
            (FINAL, SNAR, 2),
            (PASS, SUP[0], 1),
            (PASS, SFIRST[0], 0),
            (PASS, SUP[0], 3),
            (PASS, SFIRST[1], 0),
            (FINAL, SUP[0], 2),
            (PASS, SFIRST[2], 0),
            (PASS, SUP[1], 0),
            (PAIRED, GSMALL, 2),
            (ALONG, GSMALL, 1),
            (PASS, SUP[1], 3),
            (PASS, SUP[1], 1),
            (ALONG, GSMALL, 0),
            (FINAL, SUP[1], 2),
            (ALONG, GSMALL, 3),
            (PASS, SQKV[0], 3),
            (PASS, SQKV[0], 0),
            (PASS, SQKV[0], 1),
            (FINAL, SQKV[0], 2),
            (PASS, SQKV[1], 3),
            (PASS, SQKV[1], 0),
            (PASS, SQKV[1], 1),
            (FINAL, SQKV[1], 2),
            (PASS, SQKV[2], 3),
            (PASS, SQKV[2], 0),
            (PASS, SQKV[2], 1),
            (FINAL, SQKV[2], 2),
        ),
        (
            (PASS, SFIRST[1], 0),
            (FINAL, SNAR, 3),
            (PASS, SFIRST[2], 0),
            (PASS, SUP[1], 1),
            (PASS, SUP[1], 2),
            (PAIRED, GSMALL, 3),
            (FINAL, SUP[0], 3),
            (PASS, SQKV[0], 0),
            (ALONG, GSMALL, 2),
            (ALONG, GSMALL, 1),
            (PASS, SQKV[0], 1),
            (PASS, SQKV[0], 2),
            (FINAL, SUP[1], 3),
            (ALONG, GSMALL, 0),
            (PASS, SQKV[1], 0),
            (PASS, SQKV[1], 1),
            (FINAL, SQKV[0], 3),
            (PASS, SQKV[1], 2),
            (PASS, SQKV[2], 0),
            (FINAL, SQKV[1], 3),
            (PASS, SQKV[2], 1),
            (PASS, SQKV[2], 2),
            (FINAL, SQKV[2], 3),
        ),
    ),
}


def mm(left, right, left_dim, right_dim):
    return lax.dot_general(
        left, right, (((left_dim,), (right_dim,)), ((), ())), preferred_element_type=F32
    )


def span(start, size, multiple):
    return pl.ds(pl.multiple_of(start, multiple), size)


def by_eights(values):
    rows, cols = values.shape
    return jnp.sum(values.reshape(rows // 8, 8, cols), axis=0)


class Sizes:
    def __init__(self, x, wide_own, narrow_own, heads):
        self.micro, self.own, self.d = x.shape
        self.seq = 2 * self.own
        self.heads = heads
        self.dt = self.heads * 64
        self.ft = 2 * self.d
        self.wr = self.d // 8
        self.nr = narrow_own.shape[0]
        self.wc = 3 * self.dt + self.ft
        self.tiles = self.wc // LANE
        self.tokens = self.micro * self.seq


def layer_kernel(sz, *refs):
    (
        x_in, cot_in, lens, glob, steps, rand_in, b_inner, b_first, b_second, b_anchor,
        n_inner, n_first, n_second, n_anchor, w_lin, w_nar,
        f_lin, s_lin, a_lin, f_nar, s_nar, a_nar,
        out_ref, ingrad_ref, glin_out, gnar_out, mlin_out, mnar_out, small_out,
        wide, nar, xf, cot, qkv, mix, dmix, lse, mask, blocks,
        ps, pr, normed, scal, in2, uu, zb, drb, res, stage,
        gw, gn, xw, xn, zw, zn, glin, gnar, mlin, mnar, wn32,
        dsw, dsn, drw, drn, sm_all, sums, sums_x, sums_z, sm_mine, sm_peer, bias_row, norm_row, acc_b, acc_n,
        rand, corr, n_state, y_small, y_peer, s_out,
        gsend, grecv, xs, xr, zs, zr, core_s, core_r, ys, yr, loc, line_s, line_r,
    ) = refs
    z, x = place()
    shard = z * 2 + x
    t = lax.axis_index("tensor")
    near = neighbours()
    D, DT, FT, OWN, SEQ, WR, NR = sz.d, sz.dt, sz.ft, sz.own, sz.seq, sz.wr, sz.nr
    QC = 3 * DT
    base = 3 * sz.tiles * WR
    tiles_n = D // LANE
    own_at = span(t * OWN, OWN, OWN)
    peer_at = span((1 - t) * OWN, OWN, OWN)

    def local(src, dst, sem):
        return pltpu.make_async_copy(src, dst, loc.at[sem])

    loads = [
        local(w_lin, uu.at[pl.ds(0, sz.tiles * WR)], 0),
        local(w_nar, wn32, 1),
        local(x_in.at[0], xf.at[0, own_at], 2),
        local(x_in.at[1], xf.at[1, own_at], 3),
        local(cot_in, cot, 4),
    ]
    for copy in loads:
        copy.start()
    greet()

    def halves(g):
        return pl.ds(0, QC) if g == GQKV else pl.ds(QC, FT)

    def view(g, s):
        if g == GNAR:
            return nar.at[span(s * NR, NR, NR)]
        if g == GSMALL:
            return sm_all.at[s]
        return wide.at[span(s * WR, WR, WR), halves(g)]

    gat = Gather(view, gsend, grecv, (GQKV,))

    def part(g):
        return pl.ds(g * DT, DT) if g < 3 else pl.ds(QC + (g - 3) * (FT // 2), FT // 2)

    def tiles(g):
        return (g * DT // LANE, (g + 1) * DT // LANE) if g < 3 else (
            (QC + (g - 3) * (FT // 2)) // LANE, (QC + (g - 2) * (FT // 2)) // LANE)

    def source(g, s):
        if g == SNAR:
            return gn.at[span(s * NR, NR, NR)]
        if g > SNAR:
            return gn.at[span(s * NR + (g - SNAR - 1) * (NR // 3), NR // 3, 16)]
        return gw.at[span(s * WR, WR, WR), part(g)]

    def landing(wide_buf, narrow_buf):
        def at(g, slot):
            if g == SNAR:
                return narrow_buf.at[slot]
            if g > SNAR:
                return narrow_buf.at[slot, pl.ds((g - SNAR - 1) * (NR // 3), NR // 3)]
            return wide_buf.at[slot, :, part(g)]

        return at

    sca = Scatter(source, landing(xw, xn), landing(zw, zn), xs, xr, zs, zr, SUP, ROWS_OF)
    each_row = lambda run: [pl.when(z == zc)(lambda: run(zc)) for zc in range(ZS)]

    def across(g, rows=range(ZS)):
        each_row(lambda zc: gat.across(zc, g, rows))

    def sums_over():
        return pltpu.make_async_remote_copy(
            src_ref=sums, dst_ref=sums_x, send_sem=line_s.at[0], recv_sem=line_r.at[ZS],
            device_id=near["x"], device_id_type=MESH,
        )

    def sums_along(row, way):
        return pltpu.make_async_remote_copy(
            src_ref=sums_z.at[row], dst_ref=sums_z.at[row], send_sem=line_s.at[1 + row * 2 + (way == "up")],
            recv_sem=line_r.at[row], device_id=near[way], device_id_type=MESH,
        )

    def sums_ways(zc, row):
        if row == zc:
            return [way for way, ok in (("up", zc < ZS - 1), ("down", zc > 0)) if ok]
        return [onward(zc, row)] if onward(zc, row) else []

    def event(zc, kind, g, row, settled):
        if kind == BEGIN:
            gat.own(zc, g)
        elif kind == RELAY:
            gat.relay(zc, g, row)
        elif kind == CROSS:
            gat.cross(g, row)
        elif kind == PASS:
            sca.pass_on(zc, g, row)
        elif kind == MERGE:
            sca.merge(g, row)
        elif kind == FINAL:
            settle(zc, g)
            settled.append(g)
        elif kind == PAIRED:
            sums_over().wait_recv()
            sums_z[zc] = sums[...] + sums_x[...]
        else:
            sums_along(row, "up").wait_recv()
        if kind >= PAIRED:
            for way in sums_ways(zc, row):
                sums_along(row, way).start()

    settled_before = {zc: [] for zc in range(ZS)}

    def serve(name):
        def run(zc):
            for kind, group, row in PLAN[name][zc]:
                event(zc, kind, group, row, settled_before[zc])

        if name in PLAN:
            for zc in range(ZS):
                if PLAN[name][zc]:
                    pl.when(z == zc)(lambda: run(zc))

    def adam_wide(weight, grad, first, second, anchor, lanes):
        first = BETA_ONE * first + (1.0 - BETA_ONE) * grad
        second = BETA_TWO * second + (1.0 - BETA_TWO) * grad * grad
        weight = weight - LEARN_RATE * (
            (first * corr[0:1, lanes]) / (jnp.sqrt(second * corr[1:2, lanes]) + ADAM_EPS)
            + DECAY_RATE * weight
        )
        return anchor - weight

    def adam(*values):
        return adam_wide(*values, slice(None)).astype(BF16)

    def total_of(parts, at):
        value = parts[0][:, at].astype(F32)
        for other in parts[1:]:
            value = value + other[:, at].astype(F32)
        return value

    def narrow_rows(g):
        return pl.ds(0, NR) if g == SNAR else pl.ds((g - SNAR - 1) * (NR // 3), NR // 3)

    def y_copy(g):
        if g >= SNAR:
            src, dst = dsn.at[narrow_rows(g)], drn.at[narrow_rows(g)]
        else:
            src, dst = dsw.at[:, part(g)], drw.at[:, part(g)]
        return pltpu.make_async_remote_copy(
            src_ref=src, dst_ref=dst, send_sem=ys.at[g], recv_sem=yr.at[g],
            device_id=near["group"], device_id_type=MESH,
        )

    def settle(zc, g):
        parts = sca.arrived(zc, g)
        if g >= SNAR:
            rows = narrow_rows(g)
            first_row, size = (0, NR) if g == SNAR else ((g - SNAR - 1) * (NR // 3), NR // 3)

            def body(c, _):
                at = span(c * LANE, LANE, LANE)
                grad = total_of(parts, at)
                gnar[rows, at] = grad
                dsn[rows, at] = adam(
                    wn32[rows, at],
                    grad,
                    *(uu[span(base + (n * tiles_n + c) * NR + first_row, size, 8), :] for n in range(3)),
                )
                return 0

            lax.fori_loop(0, tiles_n, body, 0)
        else:
            lo, hi = tiles(g)

            def body(c, _):
                at = span(c * LANE, LANE, LANE)
                here = span((c - lo) * LANE, LANE, LANE)
                lin = pl.ds(c, WR, stride=sz.tiles)
                grad = total_of(parts, here)
                weight = glin[lin, :]
                dsw[:, at] = adam(
                    weight,
                    grad,
                    *(uu[pl.ds(n * sz.tiles * WR + c, WR, stride=sz.tiles), :] for n in range(3)),
                )
                glin[lin, :] = grad
                return 0

            lax.fori_loop(lo, hi, body, 0)
        y_copy(g).start()

    def average(g):
        y_copy(g).wait()
        if g >= SNAR:
            rows = narrow_rows(g)
            mnar[rows, :] = 0.5 * (dsn[rows, :].astype(F32) + drn[rows, :].astype(F32))
            return

        def body(c, _):
            at = span(c * LANE, LANE, LANE)
            mlin[pl.ds(c, WR, stride=sz.tiles), :] = 0.5 * (
                dsw[:, at].astype(F32) + drw[:, at].astype(F32)
            )
            return 0

        lax.fori_loop(*tiles(g), body, 0)

    def core_copy(stage_at, src, dst):
        return pltpu.make_async_remote_copy(
            src_ref=src, dst_ref=dst, send_sem=core_s.at[stage_at], recv_sem=core_r.at[stage_at],
            device_id=near["core"], device_id_type=MESH,
        )

    def rows_copy(kind, m, ref):
        return core_copy(kind * 2 + m, ref.at[span(m * SEQ + t * OWN, OWN, OWN)],
                         ref.at[span(m * SEQ + t * OWN, OWN, OWN)])

    def part_copy(kind, m):
        return core_copy(kind * 2 + m, ps.at[m], pr.at[m])

    def x_copy(m):
        return core_copy(m, x_in.at[m], xf.at[m, own_at])

    nb = bias_row.shape[1] // LANE
    bias_len, rows_len = b_inner.shape[1], n_inner.shape[2]
    rows_at = (shard * 2 + t) * rows_len
    acc_b[...] = jnp.zeros_like(acc_b)
    acc_n[...] = jnp.zeros_like(acc_n)
    sm_mine[...] = jnp.zeros_like(sm_mine)
    acc_b[0:1, 0:bias_len] = b_inner[...]
    for r in range(6):
        acc_n[0, r : r + 1, 0:rows_len] = n_inner[r]
    placed = pltpu.roll(acc_b[...], shard * bias_len, 1)
    for c in range(nb):
        sm_mine[c : c + 1, :] = placed[0:1, c * LANE : (c + 1) * LANE]
    placed = pltpu.roll(acc_n[0], rows_at, 1)
    for r in range(6):
        for c in range(tiles_n):
            at = nb + r * tiles_n + c
            sm_mine[at : at + 1, :] = placed[r : r + 1, c * LANE : (c + 1) * LANE]
    sm_all[shard] = sm_mine[...].astype(BF16)
    loads[0].wait()

    def cast_tiles(lo, hi):
        def body(c, _):
            wide[span(shard * WR, WR, WR), span(c * LANE, LANE, LANE)] = uu[
                pl.ds(c, WR, stride=sz.tiles), :
            ].astype(BF16)
            return 0

        lax.fori_loop(lo, hi, body, 0)

    cast_tiles(0, QC // LANE)
    barrier_wait()
    serve(AT_CAST)
    for m in range(2):
        x_copy(m).start()
    loads[1].wait()
    nar[span(shard * NR, NR, NR), :] = wn32[...].astype(BF16)
    cast_tiles(QC // LANE, sz.tiles)
    serve(AT_MASKS)

    for at, ref in enumerate((n_inner, n_first, n_second, n_anchor)):
        for r in range(6):
            n_state[at, r : r + 1, 0:rows_len] = ref[r]
    y_small[...] = jnp.zeros_like(y_small)
    s_out[...] = jnp.zeros_like(s_out)
    number = jnp.full((1, LANE), steps[0].astype(F32))
    corr[0:1, :] = 1.0 / (1.0 - jnp.exp(number * LOG_ONE))
    corr[1:2, :] = 1.0 / (1.0 - jnp.exp(number * LOG_TWO))
    rand[...] = jnp.full(rand.shape, -1, jnp.int32)
    for at in range(sz.micro * sz.heads):
        for r in range(3):
            rand[at, r : r + 1, 0 : rand_in.shape[2]] = rand_in[at * 3 + r]

    def build_masks():
        keys = lax.broadcasted_iota(jnp.int32, (SEQ, LANE), 0)
        lanes = lax.broadcasted_iota(jnp.int32, (SEQ, LANE), 1)
        kb = keys // 64
        blocks[...] = (kb == lanes).astype(F32).astype(BF16)
        for m in range(2):
            g0, g1 = glob[m, 0], glob[m, 1]
            base = (jnp.abs(kb - lanes) <= 1) | (kb == g0) | (kb == g1) | (lanes == g0) | (lanes == g1)
            real = keys < lens[m]

            def body(h, _):
                rows = rand[m * sz.heads + h]
                hit = base
                for r in range(3):
                    hit = hit | (kb == rows[r : r + 1, :])
                mask[m * sz.heads + h] = jnp.where(hit & real, 0.0, MASKED).astype(BF16)
                return 0

            lax.fori_loop(0, sz.heads, body, 0)

    build_masks()
    serve(AT_SMALLS)

    across(GSMALL)
    total = sm_all[0].astype(F32)
    for s in range(1, 8):
        total = total + sm_all[s].astype(F32)
    sm_mine[...] = total

    def small_copy():
        return core_copy(2, sm_mine, sm_peer)

    small_copy().start()
    small_copy().wait_recv()
    for c in range(nb):
        bias_row[0:1, c * LANE : (c + 1) * LANE] = sm_mine[c : c + 1, :]
    both = sm_mine[...] + sm_peer[...]
    for r in range(6):
        for c in range(D // LANE):
            at = nb + r * (D // LANE) + c
            norm_row[r : r + 1, c * LANE : (c + 1) * LANE] = both[at : at + 1, :]
    acc_b[...] = jnp.zeros_like(acc_b)
    acc_n[...] = jnp.zeros_like(acc_n)

    serve(AT_QKV)
    across(GQKV)
    for m in range(2):
        if m == 1:
            serve(AT_QKV + 1)
        loads[2 + m].wait()
        x_copy(m).wait_recv()
        for c in range(3):
            value = mm(xf[m], wide[:, c * DT : (c + 1) * DT], 1, 0)
            if c != 1:
                lo = 0 if c == 0 else DT
                value = value + bias_row[0:1, lo : lo + DT]
            qkv[m, :, c * DT : (c + 1) * DT] = value.astype(BF16)

    lane_low = lax.broadcasted_iota(jnp.int32, (1, LANE), 1) < 64

    def half(value, hh):
        return jnp.where(lane_low if hh == 0 else jnp.logical_not(lane_low), value, jnp.zeros_like(value))

    def pair_loads(m, p):
        return [qkv[m, :, span(c * DT + p * LANE, LANE, LANE)] for c in range(3)]

    def scores(m, p, hh, q, kh):
        head = m * sz.heads + p * 2 + hh
        kx = jnp.concatenate([kh, mask[head]], axis=1)
        qx = jnp.concatenate([q * jnp.asarray(0.125, BF16), blocks[...]], axis=1)
        return mm(kx, qx, 1, 1), head

    def attend(m):
        def body(p):
            q, k, v = pair_loads(m, p)
            out_t = jnp.zeros((LANE, SEQ), F32)
            for hh in range(2):
                s, head = scores(m, p, hh, q, half(k, hh))
                top = jnp.max(s, axis=0, keepdims=True)
                e = jnp.exp(s - top)
                total_e = jnp.sum(e, axis=0, keepdims=True)
                prob = (e * (1.0 / total_e)).astype(BF16)
                lse[head] = jnp.broadcast_to(top + jnp.log(total_e), (8, SEQ))
                out_t = out_t + mm(half(v, hh), prob, 0, 0)
            mix[span(m * SEQ, SEQ, SEQ), span(p * LANE, LANE, LANE)] = jnp.transpose(out_t).astype(BF16)

        for p in range(sz.heads // 2):
            serve(AT_ATTEND + m * (sz.heads // 2) + p)
            body(p)

    attend(0)
    attend(1)
    serve(AT_BRANCH)

    def branch(m, left, right, right_dim, kind, add):
        value = mm(left[span(m * SEQ + (1 - t) * OWN, OWN, OWN), :], right, 1, right_dim)
        ps[m] = value
        part_copy(PARTS[kind], m).start()
        value = mm(left[span(m * SEQ + t * OWN, OWN, OWN), :], right, 1, right_dim)
        if add:
            res[m] += value
        else:
            res[m] = value

    across(GNAR, [0])
    for m in range(2):
        branch(m, mix, nar[0:DT, :], 0, 0, False)

    def rows_loop(body):
        lax.fori_loop(0, OWN // 64, lambda i, c: (body(span(i * 64, 64, 64), i * 64), c)[1], 0)

    def stats(r):
        mean = jnp.mean(r, axis=1, keepdims=True)
        centred = r - mean
        var = jnp.mean(centred * centred, axis=1, keepdims=True)
        scaling = lax.rsqrt(var + NORM_EPS)
        return centred * scaling, scaling

    def norm(r):
        return norm_row[r : r + 1, :]

    def norm_one(m):
        part_copy(PARTS[0], m).wait()

        def body(rows, at):
            hidden = xf[m, span(t * OWN + at, 64, 64), :].astype(F32)
            n, scaling = stats(hidden + (res[m, rows, :] + pr[m, rows, :]) + norm(0))
            normed[m, rows, :] = n
            scal[m, rows, :] = scaling
            in2[span(m * SEQ + t * OWN + at, 64, 64), :] = (n * norm(2) + norm(3)).astype(BF16)

        rows_loop(body)
        rows_copy(ROWS[0], m, in2).start()

    serve(AT_NORM)
    for m in range(2):
        norm_one(m)
    serve(AT_FEED)

    across(GUP)

    def feed(m):
        rows_copy(ROWS[0], m, in2).wait()

        def body(c, _):
            value = mm(
                in2[span(m * SEQ, SEQ, SEQ), :], wide[:, span(QC + c * 256, 256, LANE)], 1, 0
            ) + bias_row[0:1, span(2 * DT + c * 256, 256, LANE)]
            square = value * value
            inner = GELU_A * value * (1.0 + GELU_B * square)
            tan = jnp.tanh(inner)
            hat = 0.5 * (1.0 + tan)
            zb[span(m * SEQ, SEQ, SEQ), span(c * 256, 256, 256)] = (value * hat).astype(BF16)
            slope = hat + 0.5 * value * (1.0 - tan * tan) * (GELU_A * (1.0 + 3.0 * GELU_B * square))
            for j in range(2):
                uu[span((c * 2 + j) * sz.tokens + m * SEQ, SEQ, SEQ), :] = slope[:, j * LANE : (j + 1) * LANE]
            return 0

        lax.fori_loop(0, FT // 512, body, 0)
        serve(AT_FEED + 1 + 2 * m)
        lax.fori_loop(FT // 512, FT // 256, body, 0)

    feed(0)
    serve(AT_FEED + 2)
    feed(1)
    serve(AT_DOWN)
    across(GNAR, [1, 2, 3])
    for m in range(2):
        branch(m, zb, nar[DT:, :], 0, 1, False)

    loads[4].wait()

    def count(kind, value):
        acc_n[kind] += by_eights(value)

    def norm_back(grad, n, scaling, gain):
        scaled = grad * gain
        return scaling * (
            scaled
            - jnp.mean(scaled, axis=1, keepdims=True)
            - n * jnp.mean(scaled * n, axis=1, keepdims=True)
        )

    def norm_two(m):
        part_copy(PARTS[1], m).wait()

        def body(rows, at):
            first = normed[m, rows, :] * norm(2) + norm(3)
            n, scaling = stats(first + (res[m, rows, :] + pr[m, rows, :]) + norm(1))
            stage[m, rows, :] = n * norm(4) + norm(5)
            token = t * OWN + at + lax.broadcasted_iota(jnp.int32, (64, 1), 0)
            grad = jnp.where(token < lens[m], cot[m, rows, :].astype(F32), 0.0)
            count(4, grad * n)
            count(5, grad)
            back = norm_back(grad, n, scaling, norm(4))
            count(1, back)
            res[m, rows, :] = back
            drb[span(m * SEQ + t * OWN + at, 64, 64), :] = back.astype(BF16)

        rows_loop(body)
        rows_copy(ROWS[1], m, drb).start()

    def out_copy(m):
        return local(stage.at[m], out_ref.at[m], 5 + m)

    for m in range(2):
        norm_two(m)
        out_copy(m).start()

    serve(AT_DOWN_GRAD)
    for m in range(2):
        rows_copy(ROWS[1], m, drb).wait()

    def down_grad(c, _):
        gn[span(DT + c * 256, 256, LANE), :] = mm(zb[:, span(c * 256, 256, 256)], drb[...], 0, 0).astype(BF16)
        return 0

    lax.fori_loop(0, FT // 256, down_grad, 0)
    sca.send(SNAR)

    def feed_back(m):
        def body(c, _):
            grad = mm(
                drb[span(m * SEQ, SEQ, SEQ), :], nar[span(DT + c * 256, 256, LANE), :], 1, 1
            )
            slope = jnp.concatenate(
                [uu[span((c * 2 + j) * sz.tokens + m * SEQ, SEQ, SEQ), :] for j in range(2)], axis=1
            )
            low = (grad * slope).astype(BF16)
            zb[span(m * SEQ, SEQ, SEQ), span(c * 256, 256, 256)] = low
            acc_b[:, span(2 * DT + c * 256, 256, LANE)] += by_eights(low.astype(F32))
            return 0

        lax.fori_loop(0, FT // 256, body, 0)

    for m in range(2):
        serve(AT_FEED_BACK + m)
        feed_back(m)
    serve(AT_UP_GRAD)

    def up_grad(c, _):
        gw[span(c * 256, 256, 256), QC:] = mm(in2[:, span(c * 256, 256, 256)], zb[...], 0, 0).astype(BF16)
        return 0

    lax.fori_loop(0, D // 256, up_grad, 0)
    sca.send(SUP[0])

    states = []
    for at, (lin, flat) in enumerate(((f_lin, f_nar), (s_lin, s_nar), (a_lin, a_nar))):
        states.append(local(lin, uu.at[pl.ds(at * sz.tiles * WR, sz.tiles * WR)], 7 + at))
        for c in range(tiles_n):
            states.append(
                local(
                    flat.at[:, pl.ds(c * LANE, LANE)],
                    uu.at[pl.ds(base + (at * tiles_n + c) * NR, NR)],
                    10 + at * tiles_n + c,
                )
            )
    states.append(local(w_lin, glin, 10 + 3 * tiles_n))
    for copy in states:
        copy.start()

    serve(AT_UP_BACK)
    for m in range(2):
        branch(m, zb, wide[:, QC:], 1, 2, True)
    serve(AT_NORM_BACK)
    for copy in states:
        copy.wait()

    def norm_one_back(m):
        part_copy(PARTS[2], m).wait()

        def body(rows, at):
            grad = res[m, rows, :] + pr[m, rows, :]
            n = normed[m, rows, :]
            count(2, grad * n)
            count(3, grad)
            back = norm_back(grad, n, scal[m, rows, :], norm(2))
            count(0, back)
            res[m, rows, :] = back
            drb[span(m * SEQ + t * OWN + at, 64, 64), :] = back.astype(BF16)

        rows_loop(body)
        rows_copy(ROWS[2], m, drb).start()

    for m in range(2):
        norm_one_back(m)
    for m in range(2):
        rows_copy(ROWS[2], m, drb).wait()
    serve(AT_OUT_GRAD)
    gn[0:DT, :] = mm(mix[...], drb[...], 0, 0).astype(BF16)
    for g in (*SFIRST, SUP[1]):
        sca.send(g)
    serve(AT_OUT_BACK)
    for m in range(2):
        dmix[span(m * SEQ, SEQ, SEQ), :] = mm(
            drb[span(m * SEQ, SEQ, SEQ), :], nar[0:DT, :], 1, 1
        ).astype(BF16)

    def attend_back(m):
        def body(p):
            q, k, v = pair_loads(m, p)
            do = dmix[span(m * SEQ, SEQ, SEQ), span(p * LANE, LANE, LANE)]
            dq_t = jnp.zeros((LANE, SEQ), F32)
            dk = jnp.zeros((SEQ, LANE), F32)
            dv = jnp.zeros((SEQ, LANE), F32)
            for hh in range(2):
                kh = half(k, hh)
                s, head = scores(m, p, hh, q, kh)
                prob = jnp.exp(s - lse[head][0:1, :])
                dp = mm(half(v, hh), do, 1, 1)
                centre = jnp.sum(prob * dp, axis=0, keepdims=True)
                ds = (prob * (dp - centre)).astype(BF16)
                dq_t = dq_t + mm(kh, ds, 0, 0)
                dk = dk + mm(ds, half(q, hh), 1, 0)
                dv = dv + mm(prob.astype(BF16), half(do, hh), 1, 0)
            for c, value in enumerate((jnp.transpose(dq_t) * 0.125, dk * 0.125, dv)):
                low = value.astype(BF16)
                qkv[m, :, span(c * DT + p * LANE, LANE, LANE)] = low
                if c != 1:
                    lo = 0 if c == 0 else DT
                    acc_b[:, span(lo + p * LANE, LANE, LANE)] += by_eights(low.astype(F32))

        for p in range(sz.heads // 2):
            serve(AT_ATTEND_BACK + m * (sz.heads // 2) + p)
            body(p)

    attend_back(0)
    attend_back(1)
    serve(AT_SUMS)

    sums[...] = jnp.zeros_like(sums)
    flat = jnp.sum(acc_b[...], axis=0, keepdims=True)
    for c in range(nb):
        sums[c : c + 1, :] = flat[:, c * LANE : (c + 1) * LANE]
    for r in range(6):
        flat = jnp.sum(acc_n[r], axis=0, keepdims=True)
        for c in range(tiles_n):
            at = nb + r * tiles_n + c
            sums[at : at + 1, :] = flat[:, c * LANE : (c + 1) * LANE]
    sums_over().start()
    serve(AT_QKV_GRAD)

    def attn_grad(c, _):
        value = mm(xf[0, :, span(c * 256, 256, 256)], qkv[0], 0, 0)
        value = value + mm(xf[1, :, span(c * 256, 256, 256)], qkv[1], 0, 0)
        gw[span(c * 256, 256, 256), 0:QC] = value.astype(BF16)
        return 0

    lax.fori_loop(0, D // 256, attn_grad, 0)
    for g in SQKV:
        sca.send(g)
    serve(AT_QKV_BACK)

    for m in range(2):
        out_copy(m).wait()

    def qkv_branch(m):
        right = wide[:, 0:QC]
        ps[m] = mm(qkv[m, peer_at, :], right, 1, 1)
        part_copy(PARTS[3], m).start()
        res[m] += mm(qkv[m, own_at, :], right, 1, 1)

    def ingrad_copy(m):
        return local(stage.at[m], ingrad_ref.at[m], 11 + 3 * tiles_n + m)

    for m in range(2):
        qkv_branch(m)
    serve(AT_INPUT_GRAD)
    for m in range(2):
        part_copy(PARTS[3], m).wait()
        stage[m] = res[m] + pr[m]
        ingrad_copy(m).start()

    def sums_copy():
        return core_copy(3, sm_mine, sm_peer)

    def y_small_copy():
        return pltpu.make_async_remote_copy(
            src_ref=y_small, dst_ref=y_peer, send_sem=ys.at[9], recv_sem=yr.at[9],
            device_id=near["group"], device_id_type=MESH,
        )

    def sums_total():
        total = sums_z[0]
        for other in range(1, ZS):
            total = total + sums_z[other]
        sm_mine[...] = total
        sums_copy().start()

    def small_update():
        sums_copy().wait()
        row_at = lax.broadcasted_iota(jnp.int32, sm_mine.shape, 0)
        total = sm_mine[...] + jnp.where(row_at >= nb, sm_peer[...], 0.0)
        for c in range(nb):
            acc_b[0:1, c * LANE : (c + 1) * LANE] = total[c : c + 1, :]
        for r in range(6):
            for c in range(tiles_n):
                at = nb + r * tiles_n + c
                acc_n[0, r : r + 1, c * LANE : (c + 1) * LANE] = total[at : at + 1, :]
        b_all = nb * LANE
        b_grad = pltpu.roll(acc_b[...], lax.rem(b_all - shard * bias_len, b_all), 1)[0:1, 0:bias_len]
        n_grad = pltpu.roll(acc_n[0], lax.rem(D - rows_at, D), 1)[:, 0:rows_len]
        s_out[0, 0:1, 0:bias_len] = b_grad
        s_out[0, 8:16, 0:rows_len] = n_grad
        one = slice(0, 1)
        y_small[0:1, 0:bias_len] = adam_wide(
            b_inner[...], b_grad, b_first[...], b_second[...], b_anchor[...], one
        )
        states_n = [n_state[at, :, 0:rows_len] for at in range(4)]
        y_small[8:16, 0:rows_len] = adam_wide(states_n[0], n_grad, *states_n[1:], one)
        y_small_copy().start()

    small_copy().wait_send()

    def rest(zc):
        settled = settled_before[zc]
        averaged = 0
        work = PLAN[AT_END][zc]
        summed = max([at for at, item in enumerate(work) if item[0] >= PAIRED], default=0)
        for at, (kind, g, row) in enumerate(work):
            event(zc, kind, g, row, settled)
            if at == summed:
                sums_total()
            if at == min(summed + 3, len(work) - 2):
                small_update()
            while len(settled) > averaged + 2:
                average(settled[averaged])
                averaged += 1
        for g in settled[averaged:]:
            average(g)

    each_row(rest)
    last = 13 + 3 * tiles_n
    ends = [
        local(glin, glin_out, last),
        local(gnar, gnar_out, last + 1),
        local(mlin, mlin_out, last + 2),
        local(mnar, mnar_out, last + 3),
    ]
    for copy in ends:
        copy.start()
    y_small_copy().wait()
    s_out[1] = 0.5 * (y_small[...] + y_peer[...])
    ends.append(local(s_out, small_out, last + 4))
    ends[-1].start()

    def drain(zc):
        for g in range(4):
            gat.drain(zc, g)
        for g in ROWS_OF:
            sca.drain(zc, g)
        for row in range(ZS):
            for way in sums_ways(zc, row):
                sums_along(row, way).wait_send()

    each_row(drain)
    sums_over().wait_send()
    for m in range(2):
        x_copy(m).wait_send()
        ingrad_copy(m).wait()
    for copy in ends:
        copy.wait()


PARTS = (2, 3, 4, 5)
ROWS = (6, 7, 8)
GELU_A = 0.7978845608028654
GELU_B = 0.044715
LOG_ONE = math.log(BETA_ONE)
LOG_TWO = math.log(BETA_TWO)


def gelu_tanh(values):
    return jax.nn.gelu(values, approximate=True)


def norm_stats(values):
    average = jnp.mean(values, axis=-1, keepdims=True)
    centred = values - average
    spread = jnp.mean(centred * centred, axis=-1, keepdims=True)
    scaling = lax.rsqrt(spread + NORM_EPS)
    return (centred * scaling, scaling)


def norm_back(grad_rows, normed, scaling, gain):
    scaled = grad_rows * gain
    return scaling * (
        scaled
        - jnp.mean(scaled, axis=-1, keepdims=True)
        - normed * jnp.mean(scaled * normed, axis=-1, keepdims=True)
    )


def rows_forward(values):
    return lax.all_gather(values, "tensor", axis=0, tiled=True)


def sum_forward(values):
    return lax.psum_scatter(values, "tensor", scatter_dimension=0, tiled=True)


def rows_backward(values):
    return lax.all_gather(values, "tensor", axis=0, tiled=True)


def sum_backward(values):
    return lax.psum_scatter(values, "tensor", scatter_dimension=0, tiled=True)


def block_mask(global_pair, random_rows, block_total):
    block_ids = jnp.arange(block_total, dtype=jnp.int32)
    nearby = jnp.abs(block_ids[:, None] - block_ids[None, :]) <= 1
    global_hit = jnp.any(block_ids[:, None] == global_pair[None, :], axis=1)
    allowed_base = nearby | global_hit[None, :] | global_hit[:, None]
    chosen = jnp.any(
        jnp.transpose(random_rows, (1, 0, 2))[:, :, None, :] == block_ids[None, None, :, None],
        axis=3,
    )
    return allowed_base[None] | chosen


def split_blocks(blocks_ok, seq_len, block_len):
    heads_dev = blocks_ok.shape[0]
    query_rows = min(seq_len, 512)
    block_count = seq_len // query_rows
    per_rows = query_rows // block_len
    mask_parts = jnp.transpose(
        blocks_ok.reshape(heads_dev, block_count, per_rows, -1), (1, 0, 2, 3)
    )
    return (mask_parts, query_rows, block_count)


def attend_forward(queries, keys_all, values_all, blocks_ok, key_ok, block_len):
    seq_len, heads_dev, head_width = queries.shape
    scaling = head_width ** (-0.5)
    mask_parts, query_rows, block_count = split_blocks(blocks_ok, seq_len, block_len)
    query_parts = queries.reshape(block_count, query_rows, heads_dev, head_width)

    def per_block(operands):
        query_part, mask_part = operands
        allowed = (
            jnp.repeat(jnp.repeat(mask_part, block_len, axis=1), block_len, axis=2)
            & key_ok[None, None, :]
        )
        scores = (
            jnp.einsum("qhd,khd->hqk", query_part, keys_all, preferred_element_type=jnp.float32)
            * scaling
        )
        masked = jnp.where(allowed, scores, MASKED)
        highest = jnp.max(masked, axis=2, keepdims=True)
        weights_exp = jnp.exp(masked - highest)
        summed = jnp.sum(weights_exp, axis=2, keepdims=True)
        prob_rows = (weights_exp / summed).astype(jnp.bfloat16)
        outputs = jnp.einsum(
            "hqk,khd->qhd", prob_rows, values_all, preferred_element_type=jnp.float32
        )
        return (outputs, (highest + jnp.log(summed))[:, :, 0])

    outputs, log_totals = lax.map(per_block, (query_parts, mask_parts))
    return (outputs.reshape(seq_len, heads_dev * head_width), log_totals)


def attend_backward(
    queries, keys_all, values_all, grad_mixed, log_totals, blocks_ok, key_ok, block_len
):
    seq_len, heads_dev, head_width = queries.shape
    scaling = head_width ** (-0.5)
    mask_parts, query_rows, block_count = split_blocks(blocks_ok, seq_len, block_len)
    query_parts = queries.reshape(block_count, query_rows, heads_dev, head_width)
    grad_parts = grad_mixed.reshape(block_count, query_rows, heads_dev, head_width)

    def per_block(running, operands):
        key_total, value_total = running
        query_part, mask_part, grad_part, total_part = operands
        allowed = (
            jnp.repeat(jnp.repeat(mask_part, block_len, axis=1), block_len, axis=2)
            & key_ok[None, None, :]
        )
        scores = (
            jnp.einsum("qhd,khd->hqk", query_part, keys_all, preferred_element_type=jnp.float32)
            * scaling
        )
        prob_rows = jnp.exp(jnp.where(allowed, scores, MASKED) - total_part[:, :, None])
        grad_probs = jnp.einsum(
            "qhd,khd->hqk", grad_part, values_all, preferred_element_type=jnp.float32
        )
        centre = jnp.sum(prob_rows * grad_probs, axis=2, keepdims=True)
        grad_scores = (prob_rows * (grad_probs - centre)).astype(jnp.bfloat16)
        query_grad = (
            jnp.einsum("hqk,khd->qhd", grad_scores, keys_all, preferred_element_type=jnp.float32)
            * scaling
        )
        key_total = (
            key_total
            + jnp.einsum(
                "hqk,qhd->khd", grad_scores, query_part, preferred_element_type=jnp.float32
            )
            * scaling
        )
        value_total = value_total + jnp.einsum(
            "hqk,qhd->khd",
            prob_rows.astype(jnp.bfloat16),
            grad_part,
            preferred_element_type=jnp.float32,
        )
        return ((key_total, value_total), query_grad)

    zeros_init = jnp.zeros(keys_all.shape, jnp.float32)
    (key_grad, value_grad), query_grad = lax.scan(
        per_block, (zeros_init, zeros_init), (query_parts, mask_parts, grad_parts, log_totals)
    )
    flat = heads_dev * head_width
    return (
        query_grad.reshape(seq_len, flat),
        key_grad.reshape(seq_len, flat),
        value_grad.reshape(seq_len, flat),
    )


def adam_step(weight, gradient, first, second, count):
    first_new = BETA_ONE * first + (1.0 - BETA_ONE) * gradient
    second_new = BETA_TWO * second + (1.0 - BETA_TWO) * gradient * gradient
    first_hat = first_new / (1.0 - BETA_ONE**count)
    second_hat = second_new / (1.0 - BETA_TWO**count)
    weight_new = weight - LEARN_RATE * (
        first_hat / (jnp.sqrt(second_hat) + ADAM_EPS) + DECAY_RATE * weight
    )
    return (weight_new, first_new, second_new)


def general_path(
    layer_input,
    out_cotangent,
    lengths,
    global_blocks,
    rand_blocks,
    inner_steps,
    wide_inner,
    wide_first,
    wide_second,
    wide_anchor,
    wide_outer,
    narrow_inner,
    narrow_first,
    narrow_second,
    narrow_anchor,
    narrow_outer,
    bias_inner,
    bias_first,
    bias_second,
    bias_anchor,
    bias_outer,
    norms_inner,
    norms_first,
    norms_second,
    norms_anchor,
    norms_outer,
):
    micro_count = layer_input.shape[0]
    row_count = layer_input.shape[2]
    layers = wide_inner.shape[1]
    tensor_count = lax.axis_size("tensor")
    seq_len = row_count * tensor_count
    block_total = rand_blocks.shape[2]
    block_len = seq_len // block_total
    heads_dev = rand_blocks.shape[3]
    model_width = layer_input.shape[3]
    head_width = model_width // (heads_dev * tensor_count)
    attn_cols = heads_dev * head_width
    own_rows = lax.axis_index("tensor") * row_count + jnp.arange(row_count, dtype=jnp.int32)
    norms_full = lax.all_gather(
        norms_inner[0].astype(jnp.bfloat16), ("dp", "tensor"), axis=2, tiled=True
    ).astype(jnp.float32)
    outs_rows = []
    grads_rows = []
    collected = []
    collected_rows = []
    for micro_index in range(micro_count):
        weights = [
            (
                lax.all_gather(
                    wide_inner[0, 0, :, 0, :].astype(jnp.bfloat16), "dp", axis=0, tiled=True
                ),
                lax.all_gather(
                    narrow_inner[0, 0, 0].astype(jnp.bfloat16), "dp", axis=0, tiled=True
                ),
                lax.all_gather(bias_inner[0, 0, 0].astype(jnp.bfloat16), "dp", axis=0, tiled=True),
            )
        ]
        length = lengths[micro_index, 0]
        key_ok = jnp.arange(seq_len, dtype=jnp.int32) < length
        row_ok = (own_rows < length).astype(jnp.float32)[:, None]
        blocks_ok = block_mask(
            global_blocks[micro_index, 0], rand_blocks[micro_index, 0], block_total
        )
        hidden = layer_input[micro_index, 0].astype(jnp.float32)
        layer_index = 0
        w_wide, w_narrow, w_bias = weights[layer_index]
        bias_rows = w_bias.astype(jnp.float32)
        norm_rows = norms_full[layer_index]
        inputs_one = rows_forward(hidden.astype(jnp.bfloat16))
        qkv_bias = jnp.concatenate(
            [
                bias_rows[:attn_cols],
                jnp.zeros((attn_cols,), jnp.float32),
                bias_rows[attn_cols : 2 * attn_cols],
            ]
        )
        qkv = (
            jnp.dot(inputs_one, w_wide[:, : 3 * attn_cols], preferred_element_type=jnp.float32)
            + qkv_bias
        ).astype(jnp.bfloat16)
        queries = qkv[:, :attn_cols].reshape(seq_len, heads_dev, head_width)
        keys_all = qkv[:, attn_cols : 2 * attn_cols].reshape(seq_len, heads_dev, head_width)
        values_all = qkv[:, 2 * attn_cols :].reshape(seq_len, heads_dev, head_width)
        mixed, log_totals = attend_forward(
            queries, keys_all, values_all, blocks_ok, key_ok, block_len
        )
        mixed = mixed.astype(jnp.bfloat16)
        branch = sum_forward(
            jnp.dot(mixed, w_narrow[:attn_cols], preferred_element_type=jnp.float32)
        )
        normed, scaling = norm_stats(hidden + branch + norm_rows[0])
        first_out = normed * norm_rows[2] + norm_rows[3]
        inputs_two = rows_forward(first_out.astype(jnp.bfloat16))
        inner_pre = (
            jnp.dot(inputs_two, w_wide[:, 3 * attn_cols :], preferred_element_type=jnp.float32)
            + bias_rows[2 * attn_cols :]
        )
        gelu_vals, gelu_pull = jax.vjp(gelu_tanh, inner_pre)
        gelu_out = gelu_vals.astype(jnp.bfloat16)
        branch_two = sum_forward(
            jnp.dot(gelu_out, w_narrow[attn_cols:], preferred_element_type=jnp.float32)
        )
        normed_two, scaling_two = norm_stats(first_out + branch_two + norm_rows[1])
        stored = [
            (
                inputs_one,
                queries,
                keys_all,
                values_all,
                mixed,
                log_totals,
                normed,
                scaling,
                inputs_two,
                gelu_pull,
                gelu_out,
                normed_two,
                scaling_two,
            )
        ]
        hidden = normed_two * norm_rows[4] + norm_rows[5]
        outs_rows.append(hidden)
        grad_rows = out_cotangent[micro_index, 0].astype(jnp.float32) * row_ok
        pieces = [None] * layers
        for layer_index in reversed(range(layers)):
            (
                inputs_one,
                queries,
                keys_all,
                values_all,
                mixed,
                log_totals,
                normed,
                scaling,
                inputs_two,
                gelu_pull,
                gelu_out,
                normed_two,
                scaling_two,
            ) = stored[layer_index]
            w_wide, w_narrow, w_bias = weights[layer_index]
            norm_rows = norms_full[layer_index]
            gain_two_grad = jnp.sum(grad_rows * normed_two, axis=0)
            shift_two_grad = jnp.sum(grad_rows, axis=0)
            residual_two = norm_back(grad_rows, normed_two, scaling_two, norm_rows[4])
            down_bias_grad = jnp.sum(residual_two, axis=0)
            full_two = rows_backward(residual_two.astype(jnp.bfloat16))
            down_grad = jnp.einsum(
                "sf,sd->fd", gelu_out, full_two, preferred_element_type=jnp.float32
            )
            gelu_grad = jnp.einsum(
                "sd,fd->sf", full_two, w_narrow[attn_cols:], preferred_element_type=jnp.float32
            )
            inner_grad = gelu_pull(gelu_grad)[0].astype(jnp.bfloat16)
            up_bias_grad = jnp.sum(inner_grad, axis=0, dtype=jnp.float32)
            up_grad = jnp.einsum(
                "sd,sf->df", inputs_two, inner_grad, preferred_element_type=jnp.float32
            )
            first_grad = residual_two + sum_backward(
                jnp.einsum(
                    "sf,df->sd",
                    inner_grad,
                    w_wide[:, 3 * attn_cols :],
                    preferred_element_type=jnp.float32,
                )
            )
            gain_one_grad = jnp.sum(first_grad * normed, axis=0)
            shift_one_grad = jnp.sum(first_grad, axis=0)
            residual_one = norm_back(first_grad, normed, scaling, norm_rows[2])
            out_bias_grad = jnp.sum(residual_one, axis=0)
            full_one = rows_backward(residual_one.astype(jnp.bfloat16))
            out_grad = jnp.einsum("sa,sd->ad", mixed, full_one, preferred_element_type=jnp.float32)
            mixed_grad = jnp.einsum(
                "sd,ad->sa", full_one, w_narrow[:attn_cols], preferred_element_type=jnp.float32
            ).astype(jnp.bfloat16)
            query_grad, key_grad, value_grad = attend_backward(
                queries,
                keys_all,
                values_all,
                mixed_grad.reshape(seq_len, heads_dev, head_width),
                log_totals,
                blocks_ok,
                key_ok,
                block_len,
            )
            qkv_grad = jnp.concatenate([query_grad, key_grad, value_grad], axis=1).astype(
                jnp.bfloat16
            )
            query_bias_grad = jnp.sum(qkv_grad[:, :attn_cols], axis=0, dtype=jnp.float32)
            value_bias_grad = jnp.sum(qkv_grad[:, 2 * attn_cols :], axis=0, dtype=jnp.float32)
            attn_weight_grad = jnp.einsum(
                "sd,sc->dc", inputs_one, qkv_grad, preferred_element_type=jnp.float32
            )
            grad_rows = residual_one + sum_backward(
                jnp.einsum(
                    "sc,dc->sd",
                    qkv_grad,
                    w_wide[:, : 3 * attn_cols],
                    preferred_element_type=jnp.float32,
                )
            )
            pieces[layer_index] = (
                jnp.concatenate([attn_weight_grad, up_grad], axis=1),
                jnp.concatenate([out_grad, down_grad], axis=0),
                jnp.concatenate([query_bias_grad, value_bias_grad, up_bias_grad]),
                jnp.stack(
                    [
                        out_bias_grad,
                        down_bias_grad,
                        gain_one_grad,
                        shift_one_grad,
                        gain_two_grad,
                        shift_two_grad,
                    ]
                ),
            )
        grads_rows.append(grad_rows)
        micro_pieces = (
            jnp.stack([item[0] for item in pieces]),
            jnp.stack([item[1] for item in pieces]),
            jnp.stack([item[2] for item in pieces]),
        )
        collected_rows.append(jnp.stack([item[3] for item in pieces]))
        collected.append(micro_pieces)
    merged = collected[0]
    for extra in collected[1:]:
        merged = jax.tree.map(jnp.add, merged, extra)
    merged_rows = collected_rows[0]
    for extra in collected_rows[1:]:
        merged_rows = merged_rows + extra
    shards = (
        lax.psum_scatter(merged[0], "dp", scatter_dimension=1, tiled=True),
        lax.psum_scatter(merged[1], "dp", scatter_dimension=1, tiled=True),
        lax.psum_scatter(merged[2], "dp", scatter_dimension=1, tiled=True),
    )
    row_shard = lax.psum_scatter(merged_rows, ("dp", "tensor"), scatter_dimension=2, tiled=True)
    grads = (
        shards[0][None, :, :, None, :],
        shards[1][None, :, None],
        shards[2][None, :, None],
        row_shard[None],
    )
    inners = (wide_inner, narrow_inner, bias_inner, norms_inner)
    firsts = (wide_first, narrow_first, bias_first, norms_first)
    seconds = (wide_second, narrow_second, bias_second, norms_second)
    anchors = (wide_anchor, narrow_anchor, bias_anchor, norms_anchor)
    outers = (wide_outer, narrow_outer, bias_outer, norms_outer)
    count = inner_steps[0].astype(jnp.float32)
    updated = [
        adam_step(inners[kind], grads[kind], firsts[kind], seconds[kind], count)
        for kind in range(4)
    ]
    diffs = tuple((anchors[kind] - updated[kind][0][0] for kind in range(4)))
    diff_sums = lax.psum((diffs[0], diffs[1], diffs[2], diffs[3]), "group")
    group_count = lax.axis_size("group")
    results = []
    for kind in range(4):
        mean_diff = diff_sums[kind] / group_count
        outer_new = OUTER_BETA * outers[kind] + mean_diff
        anchor_new = anchors[kind] - OUTER_RATE * (mean_diff + OUTER_BETA * outer_new)
        results.append(
            (grads[kind], updated[kind][1], updated[kind][2], mean_diff, outer_new, anchor_new)
        )
    layer_out = jnp.stack(outs_rows)[:, None]
    input_grad = jnp.stack(grads_rows)[:, None]
    return (
        layer_out,
        input_grad,
        results[0][0],
        results[0][1],
        results[0][2],
        results[0][3],
        results[0][4],
        results[0][5],
        results[1][0],
        results[1][1],
        results[1][2],
        results[1][3],
        results[1][4],
        results[1][5],
        results[2][0],
        results[2][1],
        results[2][2],
        results[2][3],
        results[2][4],
        results[2][5],
        results[3][0],
        results[3][1],
        results[3][2],
        results[3][3],
        results[3][4],
        results[3][5],
    )


def new_states(out, grad, mean, first, second, anchor, outer):
    out[0][...] = grad
    out[1][...] = BETA_ONE * first + (1.0 - BETA_ONE) * grad
    out[2][...] = BETA_TWO * second + (1.0 - BETA_TWO) * grad * grad
    out[3][...] = mean
    outer_new = OUTER_BETA * outer + mean
    out[4][...] = outer_new
    out[5][...] = anchor - OUTER_RATE * (mean + OUTER_BETA * outer_new)


def finish_kernel(*refs):
    ins, outs = refs[:23], refs[23:]
    new_states(outs[0:6], *(ref[...] for ref in ins[0:6]))
    new_states(outs[6:12], *(ref[...] for ref in ins[6:12]))
    step = pl.program_id(0)

    @pl.when(lax.rem(step, 3) == 0)
    def _():
        outs[12][...] = ins[12][...]
        outs[13][...] = ins[13][...]

    @pl.when(step == 0)
    def _():
        small, bias, rows = ins[14], ins[15:19], ins[19:23]
        bias_len, rows_len = bias[0].shape[1], rows[0].shape[2]
        new_states(
            outs[14:20], small[0, 0:1, 0:bias_len], small[1, 0:1, 0:bias_len], *(ref[...] for ref in bias)
        )
        for r in range(6):
            at = slice(8 + r, 9 + r)
            new_states(
                [ref.at[r] for ref in outs[20:26]],
                small[0, at, 0:rows_len],
                small[1, at, 0:rows_len],
                *(ref[r] for ref in rows),
            )


def finish(wide_set, narrow_set, rows_set, small, bias_set, norms_set):
    steps = 6
    shape = lambda arr: jax.ShapeDtypeStruct(arr.shape, F32)

    def rows_spec(arr, parts, every):
        return pl.BlockSpec((arr.shape[0] // parts, arr.shape[1]), lambda i: (i // every, 0))

    def whole(arr):
        return pl.BlockSpec(arr.shape, lambda i: (0,) * arr.ndim)

    big = [rows_spec(arr, steps, 1) for arr in (*wide_set, *narrow_set)]
    big += [rows_spec(arr, steps // 3, 3) for arr in rows_set]
    return pl.pallas_call(
        finish_kernel,
        grid=(steps,),
        in_specs=[*big, *(whole(arr) for arr in (small, *bias_set, *norms_set))],
        out_specs=[*big, *([whole(bias_set[0])] * 6), *([whole(norms_set[0])] * 6)],
        out_shape=[
            *(shape(arr) for arr in (*wide_set, *narrow_set, *rows_set)),
            *([shape(bias_set[0])] * 6),
            *([shape(norms_set[0])] * 6),
        ],
        name="finish",
    )(*wide_set, *narrow_set, *rows_set, small, *bias_set, *norms_set)


def fast_path(args):
    (
        layer_input, out_cotangent, lengths, global_blocks, rand_blocks, inner_steps,
        wide_inner, wide_first, wide_second, wide_anchor, wide_outer,
        narrow_inner, narrow_first, narrow_second, narrow_anchor, narrow_outer,
        bias_inner, bias_first, bias_second, bias_anchor, bias_outer,
        norms_inner, norms_first, norms_second, norms_anchor, norms_outer,
    ) = args
    x, cot = layer_input[:, 0], out_cotangent[:, 0]
    rand = jnp.transpose(rand_blocks[:, 0], (0, 2, 3, 1))
    heads = rand.shape[1]
    rand = rand.reshape(-1, 1, rand.shape[3])

    def lin(values):
        return values.reshape(-1, LANE)

    def flat(values):
        return values.reshape(values.shape[-2:])

    def line(values):
        return values.reshape(1, values.shape[-1])

    def lines(values):
        return values.reshape(6, 1, values.shape[-1])

    wide_set = [lin(v) for v in (wide_inner, wide_first, wide_second, wide_anchor, wide_outer)]
    narrow_set = [flat(v) for v in (narrow_inner, narrow_first, narrow_second, narrow_anchor, narrow_outer)]
    bias_set = [line(v) for v in (bias_inner, bias_first, bias_second, bias_anchor, bias_outer)]
    norms_set = [lines(v) for v in (norms_inner, norms_first, norms_second, norms_anchor, norms_outer)]
    bias_all, width = bias_inner.shape[-1] * 8, x.shape[2]
    used = (bias_all + 6 * width) // LANE
    small_shape = (used + -used % 16, LANE)
    y_shape = (16, bias_inner.shape[-1] + -bias_inner.shape[-1] % LANE)

    sz = Sizes(x, wide_set[0], narrow_set[0], heads)
    M, OWN, SEQ, D, DT, FT, WR, NR, WC = sz.micro, sz.own, sz.seq, sz.d, sz.dt, sz.ft, sz.wr, sz.nr, sz.wc
    vm = pltpu.VMEM
    deep = DT + FT
    scratch = [
        vm((D, WC), BF16),
        vm((deep, D), BF16),
        vm((M, SEQ, D), BF16),
        vm((M, OWN, D), BF16),
        vm((M, SEQ, 3 * DT), BF16),
        vm((M * SEQ, DT), BF16),
        vm((M * SEQ, DT), BF16),
        vm((M * sz.heads, 8, SEQ), F32),
        vm((M * sz.heads, SEQ, LANE), BF16),
        vm((SEQ, LANE), BF16),
        vm((M, OWN, D), F32),
        vm((M, OWN, D), F32),
        vm((M, OWN, D), F32),
        vm((M, OWN, 1), F32),
        vm((M * SEQ, D), BF16),
        vm((FT // LANE * M * SEQ, LANE), F32),
        vm((M * SEQ, FT), BF16),
        vm((M * SEQ, D), BF16),
        vm((M, OWN, D), F32),
        vm((M, OWN, D), F32),
        vm((D, WC), BF16),
        vm((deep, D), BF16),
        vm((ZS, WR, WC), BF16),
        vm((ZS, NR, D), BF16),
        vm((ZS + 2, WR, WC), BF16),
        vm((ZS + 1, NR, D), BF16),
        vm((sz.tiles * WR, LANE), F32),
        vm((NR, D), F32),
        vm((sz.tiles * WR, LANE), F32),
        vm((NR, D), F32),
        vm((NR, D), F32),
        vm((WR, WC), BF16),
        vm((NR, D), BF16),
        vm((WR, WC), BF16),
        vm((NR, D), BF16),
        vm((8, *small_shape), BF16),
        vm(small_shape, F32),
        vm(small_shape, F32),
        vm((ZS, *small_shape), F32),
        vm(small_shape, F32),
        vm(small_shape, F32),
        vm((8, bias_all), F32),
        vm((8, D), F32),
        vm((8, bias_all), F32),
        vm((6, 8, D), F32),
        vm((M * sz.heads, 8, LANE), jnp.int32),
        vm((8, LANE), F32),
        vm((4, 8, LANE), F32),
        vm(y_shape, F32),
        vm(y_shape, F32),
        vm((2, *y_shape), F32),
        DMA((4, ZS, 4)),
        DMA((4, 8)),
        DMA((9, ZS)),
        DMA((9, ZS)),
        DMA((9, ZS + 1)),
        DMA((9, ZS + 2)),
        DMA((18,)),
        DMA((18,)),
        DMA((10,)),
        DMA((10,)),
        DMA((18 + 3 * (D // LANE),)),
        DMA((1 + 2 * ZS,)),
        DMA((ZS + 1,)),
    ]
    shape = jax.ShapeDtypeStruct
    lin_shape, flat_shape = shape((sz.tiles * WR, LANE), F32), shape((NR, D), F32)
    layer_out, input_grad, glin, gnar, mlin, mnar, sums = pl.pallas_call(
        lambda *refs: layer_kernel(sz, *refs),
        out_shape=(
            shape((M, OWN, D), F32), shape((M, OWN, D), F32),
            lin_shape, flat_shape, lin_shape, flat_shape, shape((2, *y_shape), F32),
        ),
        in_specs=[
            ANY_SPEC, ANY_SPEC, SMEM_SPEC, SMEM_SPEC, SMEM_SPEC,
            *([VMEM_SPEC] * 9), *([ANY_SPEC] * 8),
        ],
        out_specs=(ANY_SPEC,) * 7,
        scratch_shapes=scratch,
        compiler_params=pltpu.CompilerParams(
            collective_id=1, has_side_effects=True, vmem_limit_bytes=BIG_VMEM
        ),
        name="layer_step",
    )(
        x, cot, lengths[:, 0], global_blocks[:, 0], inner_steps, rand, *bias_set[:4], *norms_set[:4],
        wide_set[0], narrow_set[0], *wide_set[1:4], *narrow_set[1:4],
    )

    done = finish(
        (glin, mlin, *wide_set[1:5]), (gnar, mnar, *narrow_set[1:5]),
        (layer_out.reshape(M * OWN, D), input_grad.reshape(M * OWN, D)),
        sums, bias_set[1:], norms_set[1:],
    )
    like = lambda values, kinds: [v.reshape(k.shape) for v, k in zip(values, kinds)]
    full = (M, 1, OWN, D)
    kinds = ((wide_inner, wide_anchor), (narrow_inner, narrow_anchor))
    outs = [done[12].reshape(full), done[13].reshape(full)]
    for at, (inner, anchor) in enumerate(kinds):
        outs += like(done[6 * at : 6 * at + 6], [inner] * 3 + [anchor] * 3)
    for at, (inner, anchor) in ((14, (bias_inner, bias_anchor)), (20, (norms_inner, norms_anchor))):
        outs += like(done[at : at + 6], [inner] * 3 + [anchor] * 3)
    return tuple(outs)


def on_device(*args):
    layer_input, rand_blocks, wide_inner, narrow_inner = args[0], args[4], args[6], args[11]
    heads, tokens, width = rand_blocks.shape[3], layer_input.shape[2], layer_input.shape[3]
    fits = (
        (lax.axis_size("dp"), lax.axis_size("tensor"), lax.axis_size("group")) == (8, 2, 2)
        and layer_input.shape[:2] == (2, 1)
        and wide_inner.shape[1] == 1
        and rand_blocks.shape[2] == 8
        and tokens == 256
        and width == heads * 2 * 64
        and heads % 2 == 0
        and wide_inner.shape[4] == 3 * heads * 64 + 2 * width
        and wide_inner.shape[2] % 48 == 0
        and narrow_inner.shape[3] % 48 == 0
        and width % 256 == 0
    )
    return fast_path(args) if fits else general_path(*args)


def solution(mesh):
    return jax.shard_map(
        on_device,
        mesh=mesh,
        in_specs=(
            P(None, ("group", "dp"), "tensor", None),
            P(None, ("group", "dp"), "tensor", None),
            P(None, ("group", "dp")),
            P(None, ("group", "dp"), None),
            P(None, ("group", "dp"), None, "tensor", None),
            P("group"),
            P("group", None, "dp", "tensor", None),
            P("group", None, "dp", "tensor", None),
            P("group", None, "dp", "tensor", None),
            P(None, "dp", "tensor", None),
            P(None, "dp", "tensor", None),
            P("group", None, "tensor", "dp", None),
            P("group", None, "tensor", "dp", None),
            P("group", None, "tensor", "dp", None),
            P(None, "tensor", "dp", None),
            P(None, "tensor", "dp", None),
            P("group", None, "tensor", "dp"),
            P("group", None, "tensor", "dp"),
            P("group", None, "tensor", "dp"),
            P(None, "tensor", "dp"),
            P(None, "tensor", "dp"),
            P("group", None, None, ("dp", "tensor")),
            P("group", None, None, ("dp", "tensor")),
            P("group", None, None, ("dp", "tensor")),
            P(None, None, ("dp", "tensor")),
            P(None, None, ("dp", "tensor")),
        ),
        out_specs=(
            P(None, ("group", "dp"), "tensor", None),
            P(None, ("group", "dp"), "tensor", None),
            P("group", None, "dp", "tensor", None),
            P("group", None, "dp", "tensor", None),
            P("group", None, "dp", "tensor", None),
            P(None, "dp", "tensor", None),
            P(None, "dp", "tensor", None),
            P(None, "dp", "tensor", None),
            P("group", None, "tensor", "dp", None),
            P("group", None, "tensor", "dp", None),
            P("group", None, "tensor", "dp", None),
            P(None, "tensor", "dp", None),
            P(None, "tensor", "dp", None),
            P(None, "tensor", "dp", None),
            P("group", None, "tensor", "dp"),
            P("group", None, "tensor", "dp"),
            P("group", None, "tensor", "dp"),
            P(None, "tensor", "dp"),
            P(None, "tensor", "dp"),
            P(None, "tensor", "dp"),
            P("group", None, None, ("dp", "tensor")),
            P("group", None, None, ("dp", "tensor")),
            P("group", None, None, ("dp", "tensor")),
            P(None, None, ("dp", "tensor")),
            P(None, None, ("dp", "tensor")),
            P(None, None, ("dp", "tensor")),
        ),
        check_vma=False,
    )
```
